256 devices in a mesh: lon: 32 (over z, x_lo, core), lat: 8 (over x_hi, y).
Axes of the slice: x: 4 (x_hi: 2, x_lo: 2; x = x_hi * 2 + x_lo), y: 4, z: 8, core: 2. Of those that a mesh axis runs over, the one named last changes fastest.
Arguments:
- increment: float32 [2, 512, 4096], P(None, 'lat', 'lon'), may hold values from -6 to 6
- members: bfloat16 [32, 2, 512, 4096], P(None, None, 'lat', 'lon'), may hold values from -6 to 6
- climate_spread: float32 [2, 512, 4096], P(None, 'lat', 'lon'), may hold values from 0.5 to 2
- diffusivity: float32 [512, 4096], P('lat', 'lon'), may hold values from 0.18 to 0.24
- inverse_area: float32 [512, 4096], P('lat', 'lon'), may hold values from 0.7 to 1
- land_sea: int32 [512, 4096], P('lat', 'lon'), may hold values 0 or 1
Outputs:
- ensemble_coefficients: bfloat16 [32, 2, 512, 4096], P(None, None, 'lat', 'lon')
- climate_coefficients: float32 [2, 512, 4096], P(None, 'lat', 'lon')
The draws below stay inside these ranges and needn't reach their ends.
All inputs are finite; a program needn't handle non-finite values. No bound on the sum of `land_sea` on one device may be relied on, other than what follows from the above.
Results may differ from the reference program's by a relative error of at most 0.001.
Values sent between devices are 32-bit elements; how exact they have to be, the bound alone decides.
No kernel may reach another device: no remote copies, remote signals or barrier semaphores. Data moves between devices by JAX's collectives and lax.ppermute only.
A program may use at most 64 MiB of HBM per device.

```python
import math
import jax
import jax.numpy as jnp
from jax import lax

MEMBERS = 32
STEPS = 6
NX = 4096
NY = 512


def touch_ends(drawn, stream_key, smallest, high):
    dims = drawn.shape
    index_at = [jax.random.randint(jax.random.fold_in(stream_key, axis), (), 0, dims[axis]) for axis in range(len(dims))]
    drawn = drawn.at[tuple(index_at)].set(smallest)
    longest = dims.index(max(dims))
    index_at[longest] = (index_at[longest] + 1) % dims[longest]
    return drawn.at[tuple(index_at)].set(high)


def steps_of(own_key, dims, shards, low, largest):
    loudness = 1.0
    for position, blocks in shards:
        draws = jax.random.uniform(jax.random.fold_in(jax.random.fold_in(own_key, 6), position), (blocks,), jnp.float32, low / len(shards), largest / len(shards))
        loudness = loudness * jnp.repeat(jnp.exp(draws), dims[position] // blocks).reshape((-1,) + (1,) * (len(dims) - 1 - position))
    return loudness


def gaussian(stream_key, extent, width, reach, shards=(), kind=jnp.bfloat16):
    result = width * jax.random.normal(stream_key, extent, jnp.float32)
    if shards:
        result = result * steps_of(stream_key, extent, shards, -0.22, 0.18)
    return jnp.clip(result, -reach, reach).astype(kind)


def setup_inputs(seed: int = 0) -> dict:
    key_of = jax.random.split(jax.random.key(seed), 7)
    return {
        "increment": gaussian(key_of[0], (2, NY, NX), 1.0, 6.0, ((1, 8), (2, 32)), jnp.float32),
        "members": gaussian(key_of[1], (MEMBERS, 2, NY, NX), 1.0, 6.0, ((2, 8), (3, 32))),
        "climate_spread": jnp.clip(jnp.exp(math.log(2.0) - 1.3862944 * jax.random.uniform(key_of[2], (2, NY, NX), jnp.float32) ** steps_of(key_of[2], (2, NY, NX), ((1, 8), (2, 32)), -0.2, 0.2)), 0.5, 2.0),
        "diffusivity": jnp.clip(jnp.exp(math.log(0.24) - 0.287682 * jax.random.uniform(key_of[3], (NY, NX), jnp.float32) ** steps_of(key_of[3], (NY, NX), ((0, 8), (1, 32)), -0.2, 0.2)), 0.18, 0.24),
        "inverse_area": jnp.clip(jnp.exp(math.log(1.0) - 0.35667496 * jax.random.uniform(key_of[4], (NY, NX), jnp.float32) ** steps_of(key_of[4], (NY, NX), ((0, 8), (1, 32)), -0.2, 0.2)), 0.7, 1.0),
        "land_sea": touch_ends((jax.random.randint(key_of[5], (NY, NX), 0, 8) < 7).astype(jnp.int32), jax.random.fold_in(key_of[5], 1), 0, 1),
    }


ensemble_weight = 0.8
climate_weight = 0.6

def neighbours(grid):
    east_side = jnp.roll(grid, -1, axis=1)
    west_side = jnp.roll(grid, 1, axis=1)
    north_side = jnp.concatenate([grid[1:], grid[-1:, ::-1]], axis=0)
    south_side = jnp.concatenate([jnp.zeros_like(grid[:1]), grid[:-1]], axis=0)
    return (east_side, west_side, north_side, south_side)

def reference(increment, members, climate_spread, diffusivity, inverse_area, land_sea):
    wet = land_sea.astype(jnp.float32)
    conduct = diffusivity * wet
    sides = neighbours(conduct)
    faces = [jnp.sqrt(conduct * side) for side in sides]

    def diffuse(field):
        for step_index in range(STEPS):
            scaled = inverse_area * field
            east_side, west_side, north_side, south_side = neighbours(scaled)
            field = field + faces[0] * (east_side - scaled) + faces[1] * (west_side - scaled) + faces[2] * (north_side - scaled) + faces[3] * (south_side - scaled)
        return field
    masked = increment * wet

    def one_member(member):
        product = member.astype(jnp.float32) * masked
        return (ensemble_weight * jax.vmap(diffuse)(product)).astype(jnp.bfloat16)
    ensemble = lax.map(one_member, members)
    climate = climate_weight * jax.vmap(diffuse)(climate_spread * masked)
    return (ensemble, climate)
```

```python
import functools

import jax
import jax.numpy as jnp
from jax import lax
from jax.experimental import pallas as pl
from jax.experimental.pallas import tpu as pltpu
from jax.sharding import PartitionSpec as P

STEPS = 6
ENSEMBLE_WEIGHT = 0.8
CLIMATE_WEIGHT = 0.6
ROWS = 64
LANES = 128
GROUPS = 9
STRIPS = 3
EXT = ROWS + 2 * STEPS
SLOT = 2 * STEPS
WIDE = 6 * STEPS
VMEM_LIMIT = 56 * 1024 * 1024
AXES = ("lon", "lat")


def lanes():
    return lax.broadcasted_iota(jnp.int32, (8, LANES), 1)


def gather(x, index):
    return jnp.take_along_axis(x, index, axis=1)


def vmem(n):
    return [pl.BlockSpec(memory_space=pltpu.VMEM)] * n


def call(kernel, name, outs, n_in, scratch=(), flops=0, nbytes=0):
    return pl.pallas_call(
        kernel,
        name=name,
        out_shape=[jax.ShapeDtypeStruct(s, d) for s, d in outs],
        in_specs=vmem(n_in),
        out_specs=vmem(len(outs)),
        scratch_shapes=list(scratch),
        compiler_params=pltpu.CompilerParams(vmem_limit_bytes=VMEM_LIMIT),
        cost_estimate=pl.CostEstimate(flops=flops, bytes_accessed=nbytes, transcendentals=0),
    )


def pack(mem, inc, clim, dif, inv, land, x0, msg_a, msg_b, edges):
    even = lax.rem(lax.axis_index("lat"), 2) == 0

    def tile(m, _):
        rows = pl.ds(pl.multiple_of(m * 16, 16), 16)
        wet = land[rows, :].astype(jnp.float32)
        masked = [inc[v, rows, :] * wet for v in range(2)]
        pattern = jnp.stack([ENSEMBLE_WEIGHT * masked[v] for v in range(2)] * 4)
        zero = jnp.zeros_like(wet)
        last = jnp.stack(
            [CLIMATE_WEIGHT * (clim[v, rows, :] * masked[v]) for v in range(2)]
            + [dif[rows, :] * wet, inv[rows, :]]
            + [zero] * 4
        )
        for g in range(GROUPS):
            block = last if g == 8 else mem[pl.ds(8 * g, 8), rows, :].astype(jnp.float32) * pattern
            for h in range(2):
                x0[pl.ds(m * 16 + 8 * h, 8), g] = jnp.swapaxes(block[:, 8 * h : 8 * h + 8], 0, 1)
        return 0

    lax.fori_loop(0, ROWS // 16, tile, 0)
    top, bottom = ROWS - STEPS, 0
    msg_a[...] = x0[pl.ds(jnp.where(even, top, bottom), STEPS)]
    msg_b[...] = x0[pl.ds(jnp.where(even, bottom, top), STEPS)]
    slot = lanes() // SLOT

    def edge(r, _):
        acc = jnp.zeros((8, LANES), jnp.float32)
        for g in range(GROUPS):
            place = 3 * (g % 3) + g // 3
            acc = jnp.where(slot == place, pltpu.roll(x0[r, g], STEPS + SLOT * place, 1), acc)
        edges[r] = acc
        return 0

    lax.fori_loop(0, ROWS, edge, 0, unroll=8)


def corner(p1, p2, halo, cor_a, cor_b):
    even = lax.rem(lax.axis_index("lat"), 2) == 0
    west_first = lax.rem(lax.axis_index("lon"), 2) == 1
    lane = lanes()
    from_first = (lax.rem(lane, SLOT) < STEPS) == west_first
    halo[...] = jnp.where(from_first[None], p1[...], p2[...])
    top, bottom = ROWS - STEPS, 0
    cor_a[...] = halo[pl.ds(jnp.where(even, top, bottom), STEPS)]
    cor_b[...] = halo[pl.ds(jnp.where(even, bottom, top), STEPS)]


def diffuse(x0, halo, msg_a, msg_b, cor_a, cor_b, ens, clim, first, second, edge, base, coef):
    lat = lax.axis_index("lat")
    even = lax.rem(lat, 2) == 0
    fold = lat == lax.axis_size("lat") - 1
    lane = lanes()
    in_slot = lax.rem(lane, SLOT)
    mirror = jnp.where(fold, LANES - 1 - lane, lane)
    mirror_slot = jnp.where(fold, jnp.minimum(lane + SLOT - 1 - 2 * in_slot, LANES - 1), lane)

    def take(r, _):
        first[r + STEPS, pl.ds(0, GROUPS)] = x0[r]
        edge[r + STEPS] = halo[r]
        return 0

    lax.fori_loop(0, ROWS, take, 0, unroll=4)
    for k in range(STEPS):
        src = jnp.where(fold, STEPS - 1 - k, k)
        for g in range(GROUPS):
            first[k, g] = jnp.where(even, msg_b[k, g], msg_a[k, g])
            first[STEPS + ROWS + k, g] = jnp.where(even, msg_a[k, g], gather(msg_b[src, g], mirror))
        edge[k] = jnp.where(even, cor_b[k], cor_a[k])
        edge[STEPS + ROWS + k] = jnp.where(even, cor_a[k], gather(cor_b[src], mirror_slot))

    q = lax.rem(lane, WIDE)
    part = lane // WIDE
    own_index = jnp.where(q < 3 * STEPS, jnp.maximum(q - STEPS, 0), jnp.minimum(LANES - 5 * STEPS + q, LANES - 1))
    is_halo = (q < STEPS) | (q >= 5 * STEPS)
    halo_slot = WIDE * part + jnp.where(q < STEPS, q, jnp.maximum(q - 4 * STEPS, 0))
    repeat = 2 * WIDE + q

    def strip(r, _):
        for j in range(STRIPS):
            acc = gather(edge[r], jnp.minimum(halo_slot + SLOT * j, LANES - 1))
            for k in range(3):
                own = gather(first[r, 3 * j + k], own_index)
                acc = jnp.where((part == k) & ~is_halo, own, acc)
            first[r, GROUPS + j] = acc
        for w, x in enumerate((first[r, GROUPS - 1], gather(first[r, GROUPS + STRIPS - 1], repeat))):
            base[r, 2 * w] = jnp.broadcast_to(x[2:3], (8, LANES))
            base[r, 2 * w + 1] = jnp.broadcast_to(x[3:4], (8, LANES))
        return 0

    lax.fori_loop(0, EXT, strip, 0, unroll=4)

    def coefficients(r, _):
        for w in range(2):
            con, inv = base[r, 2 * w], base[r, 2 * w + 1]
            total = jnp.zeros_like(con)
            for n, (con_n, inv_n) in enumerate(
                (
                    (pltpu.roll(con, LANES - 1, 1), pltpu.roll(inv, LANES - 1, 1)),
                    (pltpu.roll(con, 1, 1), pltpu.roll(inv, 1, 1)),
                    (base[r + 1, 2 * w], base[r + 1, 2 * w + 1]),
                    (base[r - 1, 2 * w], base[r - 1, 2 * w + 1]),
                )
            ):
                face = jnp.sqrt(con * con_n)
                total = total + face
                coef[r, 5 * w + 1 + n] = face * inv_n
            coef[r, 5 * w] = 1.0 - inv * total
        return 0

    lax.fori_loop(1, EXT - 1, coefficients, 0, unroll=2)

    for s in range(STEPS):
        src, dst = (first, second) if s % 2 == 0 else (second, first)

        def advance(r, _, src=src, dst=dst):
            for w in range(2):
                c0, c_e, c_w, c_n, c_s = [coef[r, 5 * w + n] for n in range(5)]
                for g in range(GROUPS) if w == 0 else range(GROUPS, GROUPS + STRIPS):
                    x = src[r, g]
                    dst[r, g] = (c0 * x + c_e * pltpu.roll(x, LANES - 1, 1)) + (
                        c_w * pltpu.roll(x, 1, 1) + (c_n * src[r + 1, g] + c_s * src[r - 1, g])
                    )
            return 0

        lax.fori_loop(s + 1, EXT - s - 1, advance, 0, unroll=4)
    state = first

    is_edge = (lane < STEPS) | (lane >= LANES - STEPS)
    back = jnp.where(lane < STEPS, lane + STEPS, jnp.maximum(4 * STEPS + lane - (LANES - STEPS), 0))

    def finish(m, _):
        for g in range(GROUPS):
            index = jnp.minimum(back + WIDE * (g % 3), LANES - 1)
            halves = []
            for h in range(2):
                rows = []
                for e in range(8):
                    r = m * 16 + 8 * h + e + STEPS
                    rows.append(jnp.where(is_edge, gather(state[r, GROUPS + g // 3], index), state[r, g]))
                halves.append(jnp.swapaxes(jnp.stack(rows), 0, 1))
            block = jnp.concatenate(halves, axis=1)
            rows = pl.ds(pl.multiple_of(m * 16, 16), 16)
            if g < 8:
                ens[pl.ds(8 * g, 8), rows, :] = block.astype(jnp.bfloat16)
            else:
                clim[:, rows, :] = block[:2]
        return 0

    lax.fori_loop(0, ROWS // 16, finish, 0)


def body(n_lon, n_lat, increment, members, climate_spread, diffusivity, inverse_area, land_sea):
    def place(i, l):
        return i % n_lon * n_lat + l

    def route(target):
        pairs = [(i, l, target(i, l)) for i in range(n_lon) for l in range(n_lat)]
        return [(place(i, l), place(*t)) for i, l, t in pairs if t is not None]

    def pair_b(i, l):
        if l == n_lat - 1:
            return (n_lon - 1 - i, l)
        return None if l == 0 else (i, l + 1 if l % 2 else l - 1)

    route_a = route(lambda i, l: (i, l ^ 1))
    route_b = route(pair_b)
    route_1 = route(lambda i, l: (i ^ 1, l))
    route_2 = route(lambda i, l: ((i + (1 if i % 2 else -1)) % n_lon, l))
    f32 = jnp.float32
    tile = (8, LANES)
    count = members.shape[0] * 2
    flat = members.reshape(count, ROWS, LANES)
    x0, msg_a, msg_b, edges = call(
        pack,
        "pack",
        [((ROWS, GROUPS, *tile), f32), ((STEPS, GROUPS, *tile), f32), ((STEPS, GROUPS, *tile), f32), ((ROWS, *tile), f32)],
        6,
    )(flat, increment, climate_spread, diffusivity, inverse_area, land_sea)
    p1 = lax.ppermute(edges, AXES, route_1)
    p2 = lax.ppermute(edges, AXES, route_2)
    got_a = lax.ppermute(msg_a, AXES, route_a)
    got_b = lax.ppermute(msg_b, AXES, route_b)
    halo, cor_a, cor_b = call(
        corner, "corner", [((ROWS, *tile), f32), ((STEPS, *tile), f32), ((STEPS, *tile), f32)], 2
    )(p1, p2)
    cor_a = lax.ppermute(cor_a, AXES, route_a)
    cor_b = lax.ppermute(cor_b, AXES, route_b)
    ensemble, climate = call(
        diffuse,
        "diffuse",
        [((count, ROWS, LANES), jnp.bfloat16), ((2, ROWS, LANES), f32)],
        6,
        [pltpu.VMEM((EXT, GROUPS + STRIPS, *tile), f32)] * 2
        + [pltpu.VMEM((EXT, *tile), f32), pltpu.VMEM((EXT, 4, *tile), f32), pltpu.VMEM((EXT, 10, *tile), f32)],
    )(x0, halo, got_a, got_b, cor_a, cor_b)
    return ensemble.reshape(members.shape), climate


def solution(mesh):
    return jax.shard_map(
        functools.partial(body, mesh.shape["lon"], mesh.shape["lat"]),
        mesh=mesh,
        in_specs=(
            P(None, "lat", "lon"),
            P(None, None, "lat", "lon"),
            P(None, "lat", "lon"),
            P("lat", "lon"),
            P("lat", "lon"),
            P("lat", "lon"),
        ),
        out_specs=(P(None, None, "lat", "lon"), P(None, "lat", "lon")),
        check_vma=False,
    )
```

```python
import functools

import jax
import jax.numpy as jnp
import numpy as np
from jax import lax
from jax.experimental import pallas as pl
from jax.experimental.pallas import tpu as pltpu
from jax.sharding import PartitionSpec as P

STEPS = 6
ENSEMBLE_WEIGHT = 0.8
CLIMATE_WEIGHT = 0.6
ROWS = 64
LANES = 128
GROUPS = 9
PHASES = 4
SETS = 3
SPAN = (LANES + 2 * STEPS) // PHASES
VECS = PHASES * SETS
SLOT = 2 * STEPS
EXT = ROWS + 2 * STEPS
TILE = (8, LANES)
AXES = ("lon", "lat")
F32 = jnp.float32
BF16 = jnp.bfloat16
MIB = 1024 * 1024


def tables():
    edge = np.zeros((8, LANES, LANES), np.float32)
    for g in range(8):
        for n in range(STEPS):
            edge[g, LANES - STEPS + n, SLOT * g + n] = 1
            edge[g, n, SLOT * g + STEPS + n] = 1
    into = np.zeros((SETS, LANES, PHASES, LANES), np.float32)
    for k in range(SETS):
        for c in range(LANES):
            into[k, c, (c + STEPS) % PHASES, SPAN * k + (c + STEPS) // PHASES] = 1
    into = into.reshape(SETS * LANES, PHASES * LANES)
    return [jnp.asarray(x, BF16) for x in (edge.reshape(4, 2 * LANES, LANES), into)]


def lanes():
    return lax.broadcasted_iota(jnp.int32, TILE, 1)


def gather(x, index):
    return jnp.take_along_axis(x, index, axis=1)


def dot(a, b, side=0):
    return lax.dot_general(a, b, (((1,), (side,)), ((), ())), preferred_element_type=F32)


def is_odd():
    return lax.rem(lax.axis_index("lat"), 2) == 1


def row_tile(index):
    return pl.ds(pl.multiple_of(index * 16, 16), 16)


def vmem(n):
    return [pl.BlockSpec(memory_space=pltpu.VMEM)] * n


def call(kernel, name, outs, n_in, scratch=(), limit=16, cost=(0, 0), in_specs=None, out_specs=None, aliases=None):
    return pl.pallas_call(
        kernel,
        name=name,
        out_shape=[jax.ShapeDtypeStruct(s, d) for s, d in outs],
        in_specs=in_specs or vmem(n_in),
        out_specs=out_specs or vmem(len(outs)),
        scratch_shapes=list(scratch),
        input_output_aliases=aliases or {},
        compiler_params=pltpu.CompilerParams(vmem_limit_bytes=limit * MIB),
        cost_estimate=pl.CostEstimate(flops=cost[0], bytes_accessed=cost[1], transcendentals=0),
    )


def edges(
    mem, inc, clim, dif, inv, land, table, into, msg_a, msg_b, msg_e, mem_v, src_v, into_v,
    side_rows, inc_v, clim_v, dif_v, inv_v, land_v, table_v, sem,
):
    pairs = [(inc, inc_v), (land, land_v), (clim, clim_v), (dif, dif_v), (inv, inv_v)]
    part = mem.shape[0] // 4
    pairs += [(mem.at[pl.ds(part * n, part)], mem_v.at[pl.ds(part * n, part)]) for n in range(4)]
    pairs += [(table, table_v), (into, into_v)]
    copies = [pltpu.make_async_copy(a, b, sem.at[n]) for n, (a, b) in enumerate(pairs)]
    for copy in copies:
        copy.start()
    odd = is_odd()
    lane = lanes()
    for copy in copies[:5]:
        copy.wait()
    wet = land_v[...].astype(F32)
    for v in range(2):
        masked = inc_v[v] * wet
        src_v[v] = ENSEMBLE_WEIGHT * masked
        src_v[2 + v] = CLIMATE_WEIGHT * (clim_v[v] * masked)
    src_v[4] = dif_v[...] * wet
    src_v[5] = inv_v[...]
    zero = jnp.zeros(TILE, F32)

    for side in range(2):
        cut = slice(8 * side, 8 * side + 8)
        rows = pl.ds(56 * side, 8)
        pattern = jnp.stack([src_v[0, rows], src_v[1, rows]] * 4)
        for g in range(GROUPS):
            if g < 8:
                if side == 0 and g % 2 == 0:
                    copies[5 + g // 2].wait()
                block = mem_v[8 * g : 8 * g + 8, pl.ds(48 * side, 16), :].astype(F32)[:, cut] * pattern
            else:
                block = jnp.stack([src_v[2 + n, rows] for n in range(4)] + [zero] * 4)
            block = jnp.swapaxes(block, 0, 1)
            for k in range(STEPS):
                side_rows[side, k, g] = block[7 - k if side else k]
    a_side = jnp.where(odd, 0, 1)
    msg_a[...] = side_rows[a_side]
    msg_b[...] = side_rows[1 - a_side]

    n = lax.rem(lane, SLOT)
    column = jnp.where(n < STEPS, LANES - STEPS + n, n - STEPS)
    ensemble = lane < 8 * SLOT
    climate = (lane >= 8 * SLOT) & (lane < 9 * SLOT)
    copies[9].wait()
    acc = None
    for q in range(4):
        pair = [mem_v[16 * q + 8 * j : 16 * q + 8 * j + 8].reshape(8 * ROWS, LANES) for j in range(2)]
        x = dot(jnp.concatenate(pair, axis=1), table_v[q])
        acc = x if acc is None else acc + x
    acc = acc.reshape(8, ROWS, LANES)
    for m in range(ROWS // 8):
        cut = slice(8 * m, 8 * m + 8)
        ends = [gather(src_v[f, cut], column) for f in range(6)] + [zero] * 4
        block = [
            jnp.where(ensemble, acc[f, cut] * ends[f % 2], jnp.where(climate, ends[2 + f], 0.0)) for f in range(8)
        ]
        block = jnp.swapaxes(jnp.stack(block), 0, 1)
        for e in range(8):
            r = 8 * m + e
            msg_e[jnp.where(odd, r, ROWS - 1 - r)] = block[e]
    copies[10].wait()


def layout(fold=False):
    lane = lanes()
    part = lane // SPAN
    out = []
    for p in range(PHASES):
        e = PHASES * (lane - SPAN * part) + p
        west, east = e < STEPS, e >= LANES + STEPS
        column = jnp.clip(e - STEPS, 0, LANES - 1)
        n = jnp.where(west, e, jnp.clip(e - LANES, 0, SLOT - 1))
        column = jnp.where(fold, LANES - 1 - column, column)
        n = jnp.where(fold, SLOT - 1 - n, n)
        out.append((column, west | east, jnp.minimum(SLOT * part + n, LANES - 1 - 2 * SETS * SLOT)))
    return out


def spread(mem, src, table, state):
    odd = is_odd()
    part = lanes() // SPAN
    places = layout()

    def tile(m, _):
        rows = row_tile(m)
        for t in range(SETS):
            n = 3 if t < 2 else 2
            lhs = [mem[pl.ds(8 * (3 * t + k), 8), rows, :].reshape(8 * 16, LANES) for k in range(n)]
            out = dot(jnp.concatenate(lhs, axis=1), table[: n * LANES, :]).reshape(8, 16, PHASES * LANES)
            for p in range(PHASES):
                column, halo, _ = places[p]
                for h in range(2):
                    cut = slice(8 * h, 8 * h + 8)
                    half = pl.ds(pl.multiple_of(m * 16 + 8 * h, 8), 8)
                    weights = [gather(src[v, half], column) for v in range(2)]
                    block = [out[f, cut, LANES * p : LANES * p + LANES] * weights[f % 2] for f in range(8)]
                    if t == 2:
                        own = (part == 2) & ~halo
                        for f in range(4):
                            block[f] = jnp.where(own, gather(src[2 + f, half], column), block[f])
                    block = jnp.swapaxes(jnp.stack(block), 0, 1)
                    for e in range(8):
                        r = m * 16 + 8 * h + e
                        state[jnp.where(odd, r, ROWS - 1 - r), PHASES * t + p] = block[e]
        return 0

    lax.fori_loop(0, ROWS // 16, tile, 0)


def corner(p1, p2, halo, cor_a, cor_b):
    west_first = lax.rem(lax.axis_index("lon"), 2) == 1
    from_first = (lax.rem(lanes(), SLOT) < STEPS) == west_first

    def row(r, _):
        halo[r] = jnp.where(from_first, p1[r], p2[r])
        return 0

    lax.fori_loop(0, ROWS, row, 0, unroll=8)
    for k in range(STEPS):
        cor_a[k] = halo[k]
        cor_b[k] = halo[ROWS - 1 - k]


def join(state, r, cor, main, places):
    part = lanes() // SPAN
    for t in range(SETS):
        for p in range(PHASES):
            column, is_halo, place = places[p]
            x = gather(cor, place + SETS * SLOT * t)
            if callable(main):
                own = main(PHASES * t + p)
            else:
                own = gather(main[3 * t], column)
                for k in (1, 2):
                    own = jnp.where(part == k, gather(main[3 * t + k], column), own)
            state[r, PHASES * t + p] = jnp.where(is_halo, x, own)


def flat(ref):
    n = 1
    for d in ref.shape[:-1]:
        n *= d
    return ref.reshape((n, LANES))


def east(x):
    return [x[p + 1] if p < PHASES - 1 else pltpu.roll(x[0], LANES - 1, 1) for p in range(PHASES)]


def west(x):
    return [x[p - 1] if p else pltpu.roll(x[PHASES - 1], 1, 1) for p in range(PHASES)]


def weigh(state, count, ground, dense, coef):
    lane = lanes()
    index = 2 * SPAN + lane - SPAN * (lane // SPAN)
    rows = flat(state)
    blocks = -(-count // 8)
    for b in range(blocks):
        for p in range(PHASES):
            for w in range(2):
                start = (8 * b * VECS + 2 * PHASES + p) * 8 + 2 + w
                x = rows[pl.ds(start, 8, stride=8 * VECS), :]
                ground[PHASES * w + p, 8 * b + 8 : 8 * b + 16, :] = gather(x, index)
    for b in range(blocks):
        con, con_a, con_b, inv, inv_a, inv_b = [
            [ground[PHASES * w + p, 8 * b + 8 + d : 8 * b + 16 + d, :] for p in range(PHASES)]
            for w in range(2)
            for d in (0, 1, -1)
        ]
        f_e = [jnp.sqrt(x * y) for x, y in zip(con, east(con))]
        f_w = west(f_e)
        i_e, i_w = east(inv), west(inv)
        for p in range(PHASES):
            f_a, f_b = jnp.sqrt(con[p] * con_a[p]), jnp.sqrt(con[p] * con_b[p])
            out = (
                1.0 - inv[p] * ((f_e[p] + f_w[p]) + (f_a + f_b)),
                f_e[p] * i_e[p],
                f_w[p] * i_w[p],
                f_a * inv_a[p],
                f_b * inv_b[p],
            )
            for n in range(5):
                dense[5 * p + n, 8 * b : 8 * b + 8, :] = out[n]

    def expand(r, _):
        for n in range(5 * PHASES):
            coef[r, n] = jnp.broadcast_to(dense[n, pl.ds(r, 1), :], TILE)
        return 0

    lax.fori_loop(1, count - 1, expand, 0, unroll=4)


def advance(row, before, after, coef, c):
    weights = [[coef[c, 5 * p + n] for n in range(5)] for p in range(PHASES)]
    out = []
    for t in range(SETS):
        x = [row(PHASES * t + p) for p in range(PHASES)]
        x_e, x_w = east(x), west(x)
        for p in range(PHASES):
            c0, c_e, c_w, c_a, c_b = weights[p]
            q = PHASES * t + p
            out.append((c0 * x[p] + c_e * x_e[p]) + (c_w * x_w[p] + (c_a * after(q) + c_b * before(q))))
    return out


def finish(row, odd, table, ens_out, clim_out, rows):
    lane = lanes()
    index = 2 * SPAN + (lane + STEPS) // PHASES
    phase = lax.rem(lane + STEPS, PHASES)
    for t in range(SETS):
        blocks = []
        for p in range(PHASES):
            halves = []
            for h in range(2):
                x = jnp.stack([row(8 * h + e, PHASES * t + p) for e in range(8)])
                halves.append(jnp.swapaxes(x, 0, 1))
            blocks.append(jnp.concatenate(halves, axis=1))
        if t == 2:
            for v in range(2):
                halves = []
                for h in range(2):
                    cut = slice(8 * h, 8 * h + 8)
                    x = gather(blocks[0][v, cut], index)
                    for p in range(1, PHASES):
                        x = jnp.where(phase == p, gather(blocks[p][v, cut], index), x)
                    halves.append(x)
                clim_out[v, rows, :] = jnp.concatenate(halves, axis=0)
        lhs = jnp.concatenate([x.astype(BF16).reshape(8 * 16, LANES) for x in blocks], axis=1)
        out = dot(lhs, table[...], 1).astype(BF16)
        for k in range(3 if t < 2 else 2):
            ens_out[pl.ds(8 * (3 * t + k), 8), rows, :] = out[:, LANES * k : LANES * k + LANES].reshape(8, 16, LANES)


NEAR = STEPS + 1
FIN = 16 - STEPS


def main(own, halo, msg_a, cor_a, table, ens, clim, near, kept, fin, first, second, ground, dense, coef):
    odd = is_odd()
    places = layout()

    def take(r, _):
        join(first, r + STEPS, halo[r], lambda q: own[r, q], places)
        return 0

    lax.fori_loop(0, ROWS, take, 0, unroll=16)
    for k in range(STEPS):
        join(first, STEPS - 1 - k, cor_a[k], [msg_a[k, g] for g in range(GROUPS)], places)
    end = STEPS + ROWS

    weigh(first, end, ground, dense, coef)
    for n in range(NEAR):
        near[n] = first[end - NEAR + n]

    for s in range(STEPS):
        src, dst = (first, second) if s % 2 == 0 else (second, first)
        if s:
            kept[s - 1, 0] = src[end - s - 2]
            kept[s - 1, 1] = src[end - s - 1]

        def step(r, _, src=src, dst=dst):
            out = advance(lambda q: src[r, q], lambda q: src[r - 1, q], lambda q: src[r + 1, q], coef, r)
            for q in range(VECS):
                dst[r, q] = out[q]
            return 0

        lax.fori_loop(s + 1, end - s - 1, step, 0, unroll=8)
    for n in range(FIN):
        fin[n] = first[end - 16 + n]

    def tile(m, _):
        src = jnp.where(odd, m, ROWS // 16 - 1 - m)

        def row(n, q):
            r = src * 16 + n
            return first[STEPS + jnp.where(odd, r, ROWS - 1 - r), q]

        finish(row, odd, table, ens, clim, row_tile(src))
        return 0

    lax.fori_loop(0, ROWS // 16 - 1, tile, 0)


def tail(near, kept, fin, msg_b, cor_b, table, ens_in, clim_in, ens, clim, one, two, ground, dense, coef, ens_rows, clim_rows, sem):
    del ens_in, clim_in
    odd = is_odd()
    fold = lax.axis_index("lat") == lax.axis_size("lat") - 1
    places = layout(fold)
    for n in range(NEAR):
        one[n] = near[n]
    for k in range(STEPS):
        join(one, NEAR + k, cor_b[k], [msg_b[k, g] for g in range(GROUPS)], places)
    weigh(one, NEAR + STEPS, ground, dense, coef)
    for s in range(STEPS):
        src, dst = (one, two) if s % 2 == 0 else (two, one)
        lo = NEAR - 1 - s
        if s:
            src[lo - 1] = kept[s - 1, 0]
            src[lo] = kept[s - 1, 1]
        for n in range(lo, lo + STEPS):
            out = advance(lambda q: src[n, q], lambda q: src[n - 1, q], lambda q: src[n + 1, q], coef, n)
            for q in range(VECS):
                dst[n, q] = out[q]
    for n in range(FIN):
        two[n] = fin[n]
    for n in range(STEPS):
        two[FIN + n] = one[1 + n]

    def row(n, q):
        return two[jnp.where(odd, n, 15 - n), q]

    finish(row, odd, table, ens_rows, clim_rows, pl.ds(0, 16))
    rows = row_tile(jnp.where(odd, ROWS // 16 - 1, 0))
    copies = [
        pltpu.make_async_copy(ens_rows, ens.at[:, rows, :], sem.at[0]),
        pltpu.make_async_copy(clim_rows, clim.at[:, rows, :], sem.at[1]),
    ]
    for copy in copies:
        copy.start()
    for copy in copies:
        copy.wait()


def body(n_lon, n_lat, increment, members, climate_spread, diffusivity, inverse_area, land_sea):
    def place(i, l):
        return i % n_lon * n_lat + l

    def route(target):
        pairs = [(i, l, target(i, l)) for i in range(n_lon) for l in range(n_lat)]
        return [(place(i, l), place(*t)) for i, l, t in pairs if t is not None]

    def pair_b(i, l):
        if l == n_lat - 1:
            return (n_lon - 1 - i, l)
        return None if l == 0 else (i, l + 1 if l % 2 else l - 1)

    route_a = route(lambda i, l: (i, l ^ 1))
    route_b = route(pair_b)
    route_1 = route(lambda i, l: (i ^ 1, l))
    route_2 = route(lambda i, l: ((i + (1 if i % 2 else -1)) % n_lon, l))
    table_edge, table_in = tables()
    count = members.shape[0] * 2
    arrays = (members.reshape(count, ROWS, LANES), increment, climate_spread, diffusivity, inverse_area, land_sea)
    side = (STEPS, GROUPS, *TILE)
    hbm = [pl.BlockSpec(memory_space=pltpu.HBM)] * 8
    two = (2, ROWS, LANES)
    msg_a, msg_b, msg_e, mem_v, src_v, into_v = call(
        edges,
        "edges",
        [(side, F32), (side, F32), ((ROWS, *TILE), F32)]
        + [((count, ROWS, LANES), BF16), ((6, ROWS, LANES), F32), (table_in.shape, BF16)],
        8,
        [pltpu.VMEM((2, *side), F32), pltpu.VMEM(two, F32), pltpu.VMEM(two, F32)]
        + [pltpu.VMEM((ROWS, LANES), d) for d in (F32, F32, jnp.int32)]
        + [pltpu.VMEM(table_edge.shape, BF16), pltpu.SemaphoreType.DMA((11,))],
        limit=12,
        in_specs=hbm,
    )(*[pltpu.with_memory_space_constraint(x, pltpu.HBM) for x in (*arrays, table_edge, table_in)])
    got_b = lax.ppermute(msg_b, AXES, route_b)
    got_a = lax.ppermute(msg_a, AXES, route_a)
    p1 = lax.ppermute(msg_e, AXES, route_1)
    p2 = lax.ppermute(msg_e, AXES, route_2)
    (own,) = call(spread, "spread", [((ROWS, VECS, *TILE), F32)], 3, limit=12)(mem_v, src_v, into_v)
    p1, p2, own = lax.optimization_barrier((p1, p2, own))
    halo, cor_a, cor_b = call(
        corner, "corner", [((ROWS, *TILE), F32), ((STEPS, *TILE), F32), ((STEPS, *TILE), F32)], 2, limit=4
    )(p1, p2)
    cor_a = lax.ppermute(cor_a, AXES, route_a)
    cor_b = lax.ppermute(cor_b, AXES, route_b)
    full = [((count, ROWS, LANES), BF16), ((2, ROWS, LANES), F32)]
    vecs = (VECS, *TILE)
    ens, clim, near, kept, fin = call(
        main,
        "main",
        full + [((NEAR, *vecs), F32), ((STEPS - 1, 2, *vecs), F32), ((FIN, *vecs), F32)],
        5,
        [pltpu.VMEM((EXT, *vecs), F32)] * 2
        + [pltpu.VMEM((n, EXT + 20, LANES), F32) for n in (2 * PHASES, 5 * PHASES)]
        + [pltpu.VMEM((EXT, 5 * PHASES, *TILE), F32)],
        limit=32,
    )(own, halo, got_a, cor_a, into_v)
    anywhere = [pl.BlockSpec(memory_space=pl.ANY)] * 2
    ens, clim = call(
        tail,
        "tail",
        full,
        8,
        [pltpu.VMEM((16, *vecs), F32)] * 2
        + [pltpu.VMEM((n, 32, LANES), F32) for n in (2 * PHASES, 5 * PHASES)]
        + [pltpu.VMEM((16, 5 * PHASES, *TILE), F32)]
        + [pltpu.VMEM((count, 16, LANES), BF16), pltpu.VMEM((2, 16, LANES), F32), pltpu.SemaphoreType.DMA((2,))],
        limit=12,
        in_specs=vmem(6) + anywhere,
        out_specs=anywhere,
        aliases={6: 0, 7: 1},
    )(near, kept, fin, got_b, cor_b, into_v, ens, clim)
    return ens.reshape(members.shape), clim


def solution(mesh):
    return jax.shard_map(
        functools.partial(body, mesh.shape["lon"], mesh.shape["lat"]),
        mesh=mesh,
        in_specs=(
            P(None, "lat", "lon"),
            P(None, None, "lat", "lon"),
            P(None, "lat", "lon"),
            P("lat", "lon"),
            P("lat", "lon"),
            P("lat", "lon"),
        ),
        out_specs=(P(None, None, "lat", "lon"), P(None, "lat", "lon")),
        check_vma=False,
    )
```

```python
import functools

import jax
import jax.numpy as jnp
import numpy as np
from jax import lax
from jax.experimental import pallas as pl
from jax.experimental.pallas import tpu as pltpu
from jax.sharding import PartitionSpec as P

STEPS = 6
ENSEMBLE_WEIGHT = 0.8
CLIMATE_WEIGHT = 0.6
ROWS = 64
LANES = 128
GROUPS = 9
PHASES = 4
SETS = 3
SPAN = (LANES + 2 * STEPS) // PHASES
VECS = PHASES * SETS
HALF = LANES // 2
EXT = ROWS + 2 * STEPS
TILE = (8, LANES)
AXES = ("lon", "lat")
F32 = jnp.float32
BF16 = jnp.bfloat16
MIB = 1024 * 1024


def tables():
    edge = np.zeros((8, LANES, LANES), np.float32)
    for g in range(8):
        for n in range(STEPS):
            edge[g, LANES - STEPS + n, STEPS * g + n] = 1
            edge[g, n, HALF + STEPS * g + n] = 1
    into = np.zeros((SETS, LANES, PHASES, LANES), np.float32)
    for k in range(SETS):
        for c in range(LANES):
            into[k, c, (c + STEPS) % PHASES, SPAN * k + (c + STEPS) // PHASES] = 1
    into = into.reshape(SETS * LANES, PHASES * LANES)
    halo = np.zeros((SETS, LANES, PHASES, LANES), np.float32)
    for g in range(GROUPS):
        for n in range(STEPS):
            for first, e in ((0, n), (HALF, LANES + STEPS + n)):
                halo[g // SETS, first + STEPS * g + n, e % PHASES, SPAN * (g % SETS) + e // PHASES] = 1
    halo = halo.reshape(SETS, LANES, PHASES * LANES)
    return [jnp.asarray(x, BF16) for x in (edge.reshape(4, 2 * LANES, LANES), into, halo)]


def lanes():
    return lax.broadcasted_iota(jnp.int32, TILE, 1)


def gather(x, index):
    return jnp.take_along_axis(x, index, axis=1)


def dot(a, b, side=0):
    return lax.dot_general(a, b, (((1,), (side,)), ((), ())), preferred_element_type=F32)


def is_odd():
    return lax.rem(lax.axis_index("lat"), 2) == 1


def row_tile(index):
    return pl.ds(pl.multiple_of(index * 16, 16), 16)


def vmem(n):
    return [pl.BlockSpec(memory_space=pltpu.VMEM)] * n


def call(kernel, name, outs, n_in, scratch=(), limit=16, cost=(0, 0), in_specs=None, out_specs=None):
    return pl.pallas_call(
        kernel,
        name=name,
        out_shape=[jax.ShapeDtypeStruct(s, d) for s, d in outs],
        in_specs=in_specs or vmem(n_in),
        out_specs=out_specs or vmem(len(outs)),
        scratch_shapes=list(scratch),
        compiler_params=pltpu.CompilerParams(vmem_limit_bytes=limit * MIB),
        cost_estimate=pl.CostEstimate(flops=cost[0], bytes_accessed=cost[1], transcendentals=0),
    )


def edges(
    mem, inc, clim, dif, inv, land, table, into, tab_h, msg_a, msg_b, msg_1, msg_2, mem_v, src_v, into_v, tab_h_v,
    side_rows, rim, inc_v, clim_v, dif_v, inv_v, land_v, table_v, sem,
):
    pairs = [(inc, inc_v), (land, land_v), (clim, clim_v), (dif, dif_v), (inv, inv_v)]
    part = mem.shape[0] // 4
    pairs += [(mem.at[pl.ds(part * n, part)], mem_v.at[pl.ds(part * n, part)]) for n in range(4)]
    pairs += [(table, table_v), (into, into_v), (tab_h, tab_h_v)]
    copies = [pltpu.make_async_copy(a, b, sem.at[n]) for n, (a, b) in enumerate(pairs)]
    for copy in copies:
        copy.start()
    odd = is_odd()
    lane = lanes()
    for copy in copies[:5]:
        copy.wait()
    wet = land_v[...].astype(F32)
    for v in range(2):
        masked = inc_v[v] * wet
        src_v[v] = ENSEMBLE_WEIGHT * masked
        src_v[2 + v] = CLIMATE_WEIGHT * (clim_v[v] * masked)
    src_v[4] = dif_v[...] * wet
    src_v[5] = inv_v[...]
    zero = jnp.zeros(TILE, F32)

    for side in range(2):
        cut = slice(8 * side, 8 * side + 8)
        rows = pl.ds(56 * side, 8)
        pattern = jnp.stack([src_v[0, rows], src_v[1, rows]] * 4)
        for g in range(GROUPS):
            if g < 8:
                if side == 0 and g % 2 == 0:
                    copies[5 + g // 2].wait()
                block = mem_v[8 * g : 8 * g + 8, pl.ds(48 * side, 16), :].astype(F32)[:, cut] * pattern
            else:
                block = jnp.stack([src_v[2 + n, rows] for n in range(4)] + [zero] * 4)
            block = jnp.swapaxes(block, 0, 1)
            for k in range(STEPS):
                side_rows[side, k, g] = block[7 - k if side else k]
    a_side = jnp.where(odd, 0, 1)
    msg_a[...] = side_rows[a_side]
    msg_b[...] = side_rows[1 - a_side]

    column = rim_column()
    ensemble = lax.rem(lane, HALF) < 8 * STEPS
    copies[9].wait()
    acc = None
    for q in range(4):
        pair = [mem_v[16 * q + 8 * j : 16 * q + 8 * j + 8].reshape(8 * ROWS, LANES) for j in range(2)]
        x = dot(jnp.concatenate(pair, axis=1), table_v[q])
        acc = x if acc is None else acc + x
    acc = acc.reshape(8, ROWS, LANES)
    for m in range(ROWS // 8):
        cut = slice(8 * m, 8 * m + 8)
        ends = [gather(src_v[f, cut], column) for f in range(6)] + [zero] * 4
        block = [
            jnp.where(ensemble, acc[f, cut] * ends[f % 2], ends[2 + f]) for f in range(8)
        ]
        block = jnp.swapaxes(jnp.stack(block), 0, 1)
        for e in range(8):
            r = 8 * m + e
            rim[jnp.where(odd, r, ROWS - 1 - r)] = block[e]
    first_east = lax.rem(lax.axis_index("lon"), 2) == 0
    low = lane < HALF
    for r in range(ROWS // 2):
        a, b = rim[r], rim[r + ROWS // 2]
        east_two = jnp.where(low, a, pltpu.roll(b, HALF, 1))
        west_two = jnp.where(low, pltpu.roll(a, HALF, 1), b)
        msg_1[r] = jnp.where(first_east, east_two, west_two)
        msg_2[r] = jnp.where(first_east, west_two, east_two)
    for copy in copies[10:]:
        copy.wait()


def rim_column():
    lane = lanes()
    n = lax.rem(lax.rem(lane, HALF), STEPS)
    return jnp.where(lane < HALF, LANES - STEPS + n, n)


def layout(fold=False):
    lane = lanes()
    part = lane // SPAN
    out = []
    for p in range(PHASES):
        e = PHASES * (lane - SPAN * part) + p
        west, east = e < STEPS, e >= LANES + STEPS
        column = jnp.clip(e - STEPS, 0, LANES - 1)
        column = jnp.where(fold, LANES - 1 - column, column)
        place = STEPS * part + jnp.where(west, e, HALF + jnp.clip(e - LANES - STEPS, 0, STEPS - 1))
        out.append((column, west | east, jnp.minimum(place, LANES - 1 - 2 * SETS * STEPS)))
    return out


def spread(mem, src, table, state):
    odd = is_odd()
    part = lanes() // SPAN
    places = layout()

    def tile(m, _):
        rows = row_tile(m)
        for t in range(SETS):
            n = 3 if t < 2 else 2
            lhs = [mem[pl.ds(8 * (3 * t + k), 8), rows, :].reshape(8 * 16, LANES) for k in range(n)]
            out = dot(jnp.concatenate(lhs, axis=1), table[: n * LANES, :]).reshape(8, 16, PHASES * LANES)
            for p in range(PHASES):
                column, halo, _ = places[p]
                for h in range(2):
                    cut = slice(8 * h, 8 * h + 8)
                    half = pl.ds(pl.multiple_of(m * 16 + 8 * h, 8), 8)
                    weights = [gather(src[v, half], column) for v in range(2)]
                    block = [out[f, cut, LANES * p : LANES * p + LANES] * weights[f % 2] for f in range(8)]
                    if t == 2:
                        own = (part == 2) & ~halo
                        for f in range(4):
                            block[f] = jnp.where(own, gather(src[2 + f, half], column), block[f])
                    block = jnp.swapaxes(jnp.stack(block), 0, 1)
                    for e in range(8):
                        r = m * 16 + 8 * h + e
                        state[jnp.where(odd, r, ROWS - 1 - r), PHASES * t + p] = block[e]
        return 0

    lax.fori_loop(0, ROWS // 16, tile, 0)


def rim_of_halo(msg_a, msg_b, rim):
    fold = lax.axis_index("lat") == lax.axis_size("lat") - 1
    group = lax.rem(lanes(), HALF) // STEPS
    column = rim_column()
    for side, msg in enumerate((msg_a, msg_b)):
        index = jnp.where(fold, LANES - 1 - column, column) if side else column
        for k in range(STEPS):
            acc = gather(msg[k, 0], index)
            for g in range(1, GROUPS):
                acc = jnp.where(group == g, gather(msg[k, g], index), acc)
            rim[side, k] = acc


def west_is_first():
    return lax.rem(lax.axis_index("lon"), 2) == 1


def join(state, r, cor, main, places):
    part = lanes() // SPAN
    for t in range(SETS):
        for p in range(PHASES):
            column, is_halo, place = places[p]
            x = gather(cor, place + SETS * STEPS * t)
            own = gather(main[3 * t], column)
            for k in (1, 2):
                own = jnp.where(part == k, gather(main[3 * t + k], column), own)
            state[r, PHASES * t + p] = jnp.where(is_halo, x, own)


def flat(ref):
    n = 1
    for d in ref.shape[:-1]:
        n *= d
    return ref.reshape((n, LANES))


def east(x):
    return [x[p + 1] if p < PHASES - 1 else pltpu.roll(x[0], LANES - 1, 1) for p in range(PHASES)]


def west(x):
    return [x[p - 1] if p else pltpu.roll(x[PHASES - 1], 1, 1) for p in range(PHASES)]


def weigh(state, count, lo, hi, ground, dense, coef, unroll):
    lane = lanes()
    index = 2 * SPAN + lane - SPAN * (lane // SPAN)
    rows = flat(state)
    blocks = -(-count // 8)
    for b in range(blocks):
        for p in range(PHASES):
            for w in range(2):
                start = (8 * b * VECS + 2 * PHASES + p) * 8 + 2 + w
                x = rows[pl.ds(start, 8, stride=8 * VECS), :]
                ground[PHASES * w + p, 8 * b + 8 : 8 * b + 16, :] = gather(x, index)
    for b in range(blocks):
        con, con_a, con_b, inv, inv_a, inv_b = [
            [ground[PHASES * w + p, 8 * b + 8 + d : 8 * b + 16 + d, :] for p in range(PHASES)]
            for w in range(2)
            for d in (0, 1, -1)
        ]
        f_e = [jnp.sqrt(x * y) for x, y in zip(con, east(con))]
        f_w = west(f_e)
        i_e, i_w = east(inv), west(inv)
        for p in range(PHASES):
            f_a, f_b = jnp.sqrt(con[p] * con_a[p]), jnp.sqrt(con[p] * con_b[p])
            out = (
                1.0 - inv[p] * ((f_e[p] + f_w[p]) + (f_a + f_b)),
                f_e[p] * i_e[p],
                f_w[p] * i_w[p],
                f_a * inv_a[p],
                f_b * inv_b[p],
            )
            for n in range(5):
                dense[5 * p + n, 8 * b : 8 * b + 8, :] = out[n]

    def expand(r, _):
        for n in range(5 * PHASES):
            coef[r, n] = jnp.broadcast_to(dense[n, pl.ds(r, 1), :], TILE)
        return 0

    lax.fori_loop(lo, hi, expand, 0, unroll=unroll)


def advance(row, before, after, coef, c):
    weights = [[coef[c, 5 * p + n] for n in range(5)] for p in range(PHASES)]
    out = []
    for t in range(SETS):
        x = [row(PHASES * t + p) for p in range(PHASES)]
        x_e, x_w = east(x), west(x)
        for p in range(PHASES):
            c0, c_e, c_w, c_a, c_b = weights[p]
            q = PHASES * t + p
            out.append((c0 * x[p] + c_e * x_e[p]) + (c_w * x_w[p] + (c_a * after(q) + c_b * before(q))))
    return out


def finish(row, odd, table, ens_out, clim_out, rows):
    lane = lanes()
    index = 2 * SPAN + (lane + STEPS) // PHASES
    phase = lax.rem(lane + STEPS, PHASES)
    for t in range(SETS):
        blocks = []
        for p in range(PHASES):
            halves = []
            for h in range(2):
                x = jnp.stack([row(8 * h + e, PHASES * t + p) for e in range(8)])
                halves.append(jnp.swapaxes(x, 0, 1))
            blocks.append(jnp.concatenate(halves, axis=1))
        if t == 2:
            for v in range(2):
                halves = []
                for h in range(2):
                    cut = slice(8 * h, 8 * h + 8)
                    x = gather(blocks[0][v, cut], index)
                    for p in range(1, PHASES):
                        x = jnp.where(phase == p, gather(blocks[p][v, cut], index), x)
                    halves.append(x)
                clim_out[v, rows, :] = jnp.concatenate(halves, axis=0)
        lhs = jnp.concatenate([x.astype(BF16).reshape(8 * 16, LANES) for x in blocks], axis=1)
        out = dot(lhs, table[...], 1).astype(BF16)
        for k in range(3 if t < 2 else 2):
            ens_out[pl.ds(8 * (3 * t + k), 8), rows, :] = out[:, LANES * k : LANES * k + LANES].reshape(8, 16, LANES)


NEAR = STEPS + 1
FIN = 16 - STEPS
CHUNK = 8


EARLY = 4


def walk(src, dst, coef, s):
    lo, hi = STEPS + s + 1, STEPS + ROWS - s - 1

    def step(n, _):
        for e in range(CHUNK):
            r = jnp.minimum(lo + n * CHUNK, hi - CHUNK) + e
            out = advance(lambda q: src[r, q], lambda q: src[r - 1, q], lambda q: src[r + 1, q], coef, r)
            for q in range(VECS):
                dst[r, q] = out[q]
        return 0

    lax.fori_loop(0, -(-(hi - lo) // CHUNK), step, 0)


def keep(kept, n, state, s):
    for d in range(2):
        kept[0, n, d] = state[STEPS + s + 1 - d]
        kept[1, n, d] = state[STEPS + ROWS - s - 2 + d]


def start(own, got_1, got_2, table, state, coef, near, kept, second, edge, ground, dense):
    west_first = west_is_first()
    low = lanes() < HALF

    def unpack(r, _):
        a, b = got_1[r], got_2[r]
        w, e = jnp.where(west_first, a, b), jnp.where(west_first, b, a)
        edge[r] = jnp.where(low, w, pltpu.roll(e, HALF, 1))
        edge[r + ROWS // 2] = jnp.where(low, pltpu.roll(w, HALF, 1), e)
        return 0

    lax.fori_loop(0, ROWS // 2, unpack, 0, unroll=8)

    def take(m, _):
        x = edge[pl.ds(m * 16, 16)].reshape(16 * 8, LANES)
        parts = []
        for _ in range(3):
            parts.append(x.astype(BF16))
            x = x - parts[-1].astype(F32)
        lhs = jnp.concatenate(parts, axis=1)
        for t in range(SETS):
            out = dot(lhs, jnp.concatenate([table[t]] * 3, axis=0)).reshape(16, 8, PHASES * LANES)
            for p in range(PHASES):
                q = PHASES * t + p
                rows = pl.ds(m * 16, 16)
                state[pl.ds(STEPS + m * 16, 16), q] = own[rows, q] + out[:, :, LANES * p : LANES * p + LANES]
        return 0

    lax.fori_loop(0, ROWS // 16, take, 0, unroll=4)
    end = STEPS + ROWS
    weigh(state, end, STEPS + 1, end - 1, ground, dense, coef, 8)
    for n in range(NEAR):
        near[0, n] = state[2 * STEPS - n]
        near[1, n] = state[end - NEAR + n]
    for s in range(EARLY):
        src, dst = (state, second) if s % 2 == 0 else (second, state)
        walk(src, dst, coef, s)
        keep(kept, s, dst, s + 1)


def main(state, coef, table, ens, clim, kept, fin, first, second):
    odd = is_odd()
    src = state
    for s in range(EARLY, STEPS):
        dst = first if s % 2 else second
        walk(src, dst, coef, s)
        if s < STEPS - 1:
            keep(kept, s - EARLY, dst, s + 1)
        src = dst
    end = STEPS + ROWS
    for n in range(FIN):
        fin[0, n] = first[STEPS + 15 - n]
        fin[1, n] = first[end - 16 + n]

    def tile(m, _):
        def row(n, q):
            r = 16 * m + 16 + n
            return first[STEPS + jnp.where(odd, r, ROWS - 1 - r), q]

        finish(row, odd, table, ens, clim, row_tile(m))
        return 0

    lax.fori_loop(0, ROWS // 16 - 2, tile, 0)


def tail(
    near, kept_a, kept_b, fin, msg_a, msg_b, rim_1, rim_2, table, ens_main, clim_main, ens, clim,
    one, two, ground, dense, coef, ens_rows, clim_rows, sem,
):
    odd = is_odd()
    done = pl.ds(16, ROWS - 32)
    copies = [
        pltpu.make_async_copy(ens_main, ens.at[:, done, :], sem.at[0]),
        pltpu.make_async_copy(clim_main, clim.at[:, done, :], sem.at[1]),
    ]
    for copy in copies:
        copy.start()
    fold = lax.axis_index("lat") == lax.axis_size("lat") - 1
    west_first = west_is_first()
    low = lanes() < HALF
    places = [layout(), layout(fold)]
    for side, msg in enumerate((msg_a, msg_b)):
        for n in range(NEAR):
            one[16 * side + n] = near[side, n]
        for k in range(STEPS):
            cor = jnp.where(low == west_first, rim_1[side, k], rim_2[side, k])
            join(one, 16 * side + NEAR + k, cor, [msg[k, g] for g in range(GROUPS)], places[side])
    weigh(one, 32, 1, 31, ground, dense, coef, 10)
    for s in range(STEPS):
        src, dst = (one, two) if s % 2 == 0 else (two, one)
        lo = NEAR - 1 - s
        kept, n = (kept_a, s - 1) if s <= EARLY else (kept_b, s - 1 - EARLY)
        for side in range(2):
            if s:
                src[16 * side + lo - 1] = kept[side, n, 0]
                src[16 * side + lo] = kept[side, n, 1]
        for side in range(2):
            for r in range(16 * side + lo, 16 * side + lo + STEPS):
                out = advance(lambda q: src[r, q], lambda q: src[r - 1, q], lambda q: src[r + 1, q], coef, r)
                for q in range(VECS):
                    dst[r, q] = out[q]
    for side in range(2):
        for n in range(FIN):
            two[16 * side + n] = fin[side, n]
        for n in range(STEPS):
            two[16 * side + FIN + n] = one[16 * side + 1 + n]
        rising = odd if side else ~odd

        def row(n, q):
            return two[16 * side + jnp.where(rising, n, 15 - n), q]

        finish(row, odd, table, ens_rows.at[side], clim_rows.at[side], pl.ds(0, 16))
        rows = row_tile(jnp.where(rising, ROWS // 16 - 1, 0))
        copies += [
            pltpu.make_async_copy(ens_rows.at[side], ens.at[:, rows, :], sem.at[2 + 2 * side]),
            pltpu.make_async_copy(clim_rows.at[side], clim.at[:, rows, :], sem.at[3 + 2 * side]),
        ]
        for copy in copies[-2:]:
            copy.start()
    for copy in copies:
        copy.wait()


def body(n_lon, n_lat, increment, members, climate_spread, diffusivity, inverse_area, land_sea):
    def place(i, l):
        return i % n_lon * n_lat + l

    def route(target):
        pairs = [(i, l, target(i, l)) for i in range(n_lon) for l in range(n_lat)]
        return [(place(i, l), place(*t)) for i, l, t in pairs if t is not None]

    def pair_b(i, l):
        if l == n_lat - 1:
            return (n_lon - 1 - i, l)
        return None if l == 0 else (i, l + 1 if l % 2 else l - 1)

    route_a = route(lambda i, l: (i, l ^ 1))
    route_b = route(pair_b)
    route_1 = route(lambda i, l: (i ^ 1, l))
    route_2 = route(lambda i, l: ((i + (1 if i % 2 else -1)) % n_lon, l))
    table_edge, table_in, table_halo = tables()
    count = members.shape[0] * 2
    arrays = (members.reshape(count, ROWS, LANES), increment, climate_spread, diffusivity, inverse_area, land_sea)
    side = (STEPS, GROUPS, *TILE)
    hbm = [pl.BlockSpec(memory_space=pltpu.HBM)] * 9
    two = (2, ROWS, LANES)
    packed = ((ROWS // 2, *TILE), F32)
    msg_a, msg_b, msg_1, msg_2, mem_v, src_v, into_v, tab_h_v = call(
        edges,
        "edges",
        [(side, F32), (side, F32), packed, packed]
        + [((count, ROWS, LANES), BF16), ((6, ROWS, LANES), F32), (table_in.shape, BF16), (table_halo.shape, BF16)],
        9,
        [pltpu.VMEM((2, *side), F32), pltpu.VMEM((ROWS, *TILE), F32), pltpu.VMEM(two, F32), pltpu.VMEM(two, F32)]
        + [pltpu.VMEM((ROWS, LANES), d) for d in (F32, F32, jnp.int32)]
        + [pltpu.VMEM(table_edge.shape, BF16), pltpu.SemaphoreType.DMA((12,))],
        limit=12,
        in_specs=hbm,
    )(*[pltpu.with_memory_space_constraint(x, pltpu.HBM) for x in (*arrays, table_edge, table_in, table_halo)])
    got_b = lax.ppermute(msg_b, AXES, route_b)
    got_a = lax.ppermute(msg_a, AXES, route_a)
    got_2 = lax.ppermute(msg_2, AXES, route_2)
    got_1 = lax.ppermute(msg_1, AXES, route_1)
    (own,) = call(spread, "spread", [((ROWS, VECS, *TILE), F32)], 3, limit=12)(mem_v, src_v, into_v)
    got_1, got_2, own = lax.optimization_barrier((got_1, got_2, own))
    vecs = (VECS, *TILE)
    state, coef, near, kept_a = call(
        start,
        "start",
        [((EXT, *vecs), F32), ((EXT, 5 * PHASES, *TILE), F32), ((2, NEAR, *vecs), F32), ((2, EARLY, 2, *vecs), F32)],
        4,
        [pltpu.VMEM((EXT, *vecs), F32), pltpu.VMEM((ROWS, *TILE), F32)]
        + [pltpu.VMEM((n, EXT + 20, LANES), F32) for n in (2 * PHASES, 5 * PHASES)],
        limit=20,
        cost=(10**11, 10**8),
    )(own, got_1, got_2, tab_h_v)
    got_a, got_b, state = lax.optimization_barrier((got_a, got_b, state))
    (rim,) = call(rim_of_halo, "rim", [((2, STEPS, *TILE), F32)], 2, limit=4)(got_a, got_b)
    rim_1 = lax.ppermute(rim, AXES, route_1)
    rim_2 = lax.ppermute(rim, AXES, route_2)
    full = [((count, ROWS, LANES), BF16), ((2, ROWS, LANES), F32)]
    most = [((count, ROWS - 32, LANES), BF16), ((2, ROWS - 32, LANES), F32)]
    ens, clim, kept_b, fin = call(
        main,
        "main",
        most + [((2, STEPS - EARLY - 1, 2, *vecs), F32), ((2, FIN, *vecs), F32)],
        3,
        [pltpu.VMEM((EXT, *vecs), F32)] * 2,
        limit=20,
        cost=(10**11, 10**8),
    )(state, coef, into_v)
    ens, clim = call(
        tail,
        "tail",
        full,
        11,
        [pltpu.VMEM((32, *vecs), F32)] * 2
        + [pltpu.VMEM((n, 48, LANES), F32) for n in (2 * PHASES, 5 * PHASES)]
        + [pltpu.VMEM((32, 5 * PHASES, *TILE), F32)]
        + [pltpu.VMEM((2, count, 16, LANES), BF16), pltpu.VMEM((2, 2, 16, LANES), F32), pltpu.SemaphoreType.DMA((6,))],
        limit=16,
        out_specs=[pl.BlockSpec(memory_space=pltpu.HBM)] * 2,
    )(near, kept_a, kept_b, fin, got_a, got_b, rim_1, rim_2, into_v, ens, clim)
    return ens.reshape(members.shape), clim


def solution(mesh):
    return jax.shard_map(
        functools.partial(body, mesh.shape["lon"], mesh.shape["lat"]),
        mesh=mesh,
        in_specs=(
            P(None, "lat", "lon"),
            P(None, None, "lat", "lon"),
            P(None, "lat", "lon"),
            P("lat", "lon"),
            P("lat", "lon"),
            P("lat", "lon"),
        ),
        out_specs=(P(None, None, "lat", "lon"), P(None, "lat", "lon")),
        check_vma=False,
    )
```

```python
import functools

import jax
import jax.numpy as jnp
import numpy as np
from jax import lax
from jax.experimental import pallas as pl
from jax.experimental.pallas import tpu as pltpu
from jax.sharding import PartitionSpec as P

STEPS = 6
ENSEMBLE_WEIGHT = 0.8
CLIMATE_WEIGHT = 0.6
ROWS = 64
LANES = 128
GROUPS = 9
PHASES = 4
SETS = 3
SPAN = (LANES + 2 * STEPS) // PHASES
VECS = PHASES * SETS
HALF = LANES // 2
EXT = ROWS + 2 * STEPS
TILE = (8, LANES)
NEAR = STEPS + 1
AXES = ("lon", "lat")
F32 = jnp.float32
BF16 = jnp.bfloat16
MIB = 1024 * 1024


def tables():
    edge = np.zeros((8, LANES, LANES), np.float32)
    for g in range(8):
        for n in range(STEPS):
            edge[g, LANES - STEPS + n, STEPS * g + n] = 1
            edge[g, n, HALF + STEPS * g + n] = 1
    into = np.zeros((SETS, LANES, PHASES, LANES), np.float32)
    for k in range(SETS):
        for c in range(LANES):
            into[k, c, (c + STEPS) % PHASES, SPAN * k + (c + STEPS) // PHASES] = 1
    into = into.reshape(SETS * LANES, PHASES * LANES)
    halo = np.zeros((SETS, LANES, PHASES, LANES), np.float32)
    for g in range(GROUPS):
        for n in range(STEPS):
            for first, e in ((0, n), (HALF, LANES + STEPS + n)):
                halo[g // SETS, first + STEPS * g + n, e % PHASES, SPAN * (g % SETS) + e // PHASES] = 1
    halo = halo.reshape(SETS, LANES, PHASES * LANES)
    return [jnp.asarray(x, BF16) for x in (edge.reshape(4, 2 * LANES, LANES), into, halo)]


def lanes():
    return lax.broadcasted_iota(jnp.int32, TILE, 1)


def gather(x, index):
    return jnp.take_along_axis(x, index, axis=1)


def dot(a, b, side=0):
    return lax.dot_general(a, b, (((1,), (side,)), ((), ())), preferred_element_type=F32)


def is_odd():
    return lax.rem(lax.axis_index("lat"), 2) == 1


def row_tile(index):
    return pl.ds(pl.multiple_of(index * 16, 16), 16)


def vmem(n):
    return [pl.BlockSpec(memory_space=pltpu.VMEM)] * n


def call(kernel, name, outs, n_in, scratch=(), limit=16, cost=(0, 0), in_specs=None, out_specs=None, aliases=None):
    return pl.pallas_call(
        kernel,
        name=name,
        out_shape=[jax.ShapeDtypeStruct(s, d) for s, d in outs],
        in_specs=in_specs or vmem(n_in),
        out_specs=out_specs or vmem(len(outs)),
        scratch_shapes=list(scratch),
        input_output_aliases=aliases or {},
        compiler_params=pltpu.CompilerParams(vmem_limit_bytes=limit * MIB),
        cost_estimate=pl.CostEstimate(flops=cost[0], bytes_accessed=cost[1], transcendentals=0),
    )


def edges(
    mem, inc, clim, dif, inv, land, table, into, tab_h, msg_a, msg_b, msg_1, msg_2, mem_v, src_v, into_v, tab_h_v, own,
    side_rows, rim, inc_v, clim_v, dif_v, inv_v, land_v, table_v, sem,
):
    pairs = [(inc, inc_v), (land, land_v), (clim, clim_v), (dif, dif_v), (inv, inv_v)]
    part = mem.shape[0] // 4
    pairs += [(mem.at[pl.ds(part * n, part)], mem_v.at[pl.ds(part * n, part)]) for n in range(4)]
    pairs += [(table, table_v), (into, into_v), (tab_h, tab_h_v)]
    copies = [pltpu.make_async_copy(a, b, sem.at[n]) for n, (a, b) in enumerate(pairs)]
    for copy in copies:
        copy.start()
    odd = is_odd()
    lane = lanes()
    for copy in copies[:5]:
        copy.wait()
    wet = land_v[...].astype(F32)
    for v in range(2):
        masked = inc_v[v] * wet
        src_v[v] = ENSEMBLE_WEIGHT * masked
        src_v[2 + v] = CLIMATE_WEIGHT * (clim_v[v] * masked)
    src_v[4] = dif_v[...] * wet
    src_v[5] = inv_v[...]
    zero = jnp.zeros(TILE, F32)

    for side in range(2):
        cut = slice(8 * side, 8 * side + 8)
        rows = pl.ds(56 * side, 8)
        pattern = jnp.stack([src_v[0, rows], src_v[1, rows]] * 4)
        for g in range(GROUPS):
            if g < 8:
                if side == 0 and g % 2 == 0:
                    copies[5 + g // 2].wait()
                block = mem_v[8 * g : 8 * g + 8, pl.ds(48 * side, 16), :].astype(F32)[:, cut] * pattern
            else:
                block = jnp.stack([src_v[2 + n, rows] for n in range(4)] + [zero] * 4)
            block = jnp.swapaxes(block, 0, 1)
            for k in range(STEPS):
                side_rows[side, k, g] = block[7 - k if side else k]
    a_side = jnp.where(odd, 0, 1)
    msg_a[...] = side_rows[a_side]
    msg_b[...] = side_rows[1 - a_side]

    column = rim_column()
    ensemble = lax.rem(lane, HALF) < 8 * STEPS
    copies[9].wait()
    acc = None
    for q in range(4):
        pair = [mem_v[16 * q + 8 * j : 16 * q + 8 * j + 8].reshape(8 * ROWS, LANES) for j in range(2)]
        x = dot(jnp.concatenate(pair, axis=1), table_v[q])
        acc = x if acc is None else acc + x
    acc = acc.reshape(8, ROWS, LANES)
    for m in range(ROWS // 8):
        cut = slice(8 * m, 8 * m + 8)
        ends = [gather(src_v[f, cut], column) for f in range(6)] + [zero] * 4
        block = [
            jnp.where(ensemble, acc[f, cut] * ends[f % 2], ends[2 + f]) for f in range(8)
        ]
        block = jnp.swapaxes(jnp.stack(block), 0, 1)
        for e in range(8):
            r = 8 * m + e
            rim[jnp.where(odd, r, ROWS - 1 - r)] = block[e]
    first_east = lax.rem(lax.axis_index("lon"), 2) == 0
    low = lane < HALF
    for r in range(ROWS // 2):
        a, b = rim[r], rim[r + ROWS // 2]
        east_two = jnp.where(low, a, pltpu.roll(b, HALF, 1))
        west_two = jnp.where(low, pltpu.roll(a, HALF, 1), b)
        msg_1[r] = jnp.where(first_east, east_two, west_two)
        msg_2[r] = jnp.where(first_east, west_two, east_two)
    for copy in copies[10:]:
        copy.wait()

    @pl.when(first_out())
    def _():
        deal(mem_v, src_v, into_v, own)


def rim_column():
    lane = lanes()
    n = lax.rem(lax.rem(lane, HALF), STEPS)
    return jnp.where(lane < HALF, LANES - STEPS + n, n)


def layout(fold=False):
    lane = lanes()
    part = lane // SPAN
    out = []
    for p in range(PHASES):
        e = PHASES * (lane - SPAN * part) + p
        west, east = e < STEPS, e >= LANES + STEPS
        column = jnp.clip(e - STEPS, 0, LANES - 1)
        column = jnp.where(fold, LANES - 1 - column, column)
        place = STEPS * part + jnp.where(west, e, HALF + jnp.clip(e - LANES - STEPS, 0, STEPS - 1))
        out.append((column, west | east, jnp.minimum(place, LANES - 1 - 2 * SETS * STEPS)))
    return out


def first_out():
    return lax.axis_index("lon") < 4


def spread(mem, src, table, before, state):
    del before

    @pl.when(~first_out())
    def _():
        deal(mem, src, table, state)


def deal(mem, src, table, state):
    odd = is_odd()
    part = lanes() // SPAN
    places = layout()

    def tile(m, _):
        rows = row_tile(m)
        for t in range(SETS):
            n = 3 if t < 2 else 2
            lhs = [mem[pl.ds(8 * (3 * t + k), 8), rows, :].reshape(8 * 16, LANES) for k in range(n)]
            out = dot(jnp.concatenate(lhs, axis=1), table[: n * LANES, :]).reshape(8, 16, PHASES * LANES)
            for p in range(PHASES):
                column, halo, _ = places[p]
                for h in range(2):
                    cut = slice(8 * h, 8 * h + 8)
                    half = pl.ds(pl.multiple_of(m * 16 + 8 * h, 8), 8)
                    weights = [gather(src[v, half], column) for v in range(2)]
                    block = [out[f, cut, LANES * p : LANES * p + LANES] * weights[f % 2] for f in range(8)]
                    if t == 2:
                        own = (part == 2) & ~halo
                        for f in range(4):
                            block[f] = jnp.where(own, gather(src[2 + f, half], column), block[f])
                    block = jnp.swapaxes(jnp.stack(block), 0, 1)
                    for e in range(8):
                        r = m * 16 + 8 * h + e
                        state[jnp.where(odd, r, ROWS - 1 - r), PHASES * t + p] = block[e]
        return 0

    lax.fori_loop(0, ROWS // 16, tile, 0)


def rim_of_halo(msg_a, msg_b, rim):
    fold = lax.axis_index("lat") == lax.axis_size("lat") - 1
    group = lax.rem(lanes(), HALF) // STEPS
    column = rim_column()
    for side, msg in enumerate((msg_a, msg_b)):
        index = jnp.where(fold, LANES - 1 - column, column) if side else column
        for k in range(STEPS):
            acc = gather(msg[k, 0], index)
            for g in range(1, GROUPS):
                acc = jnp.where(group == g, gather(msg[k, g], index), acc)
            rim[side, k] = acc


def west_is_first():
    return lax.rem(lax.axis_index("lon"), 2) == 1


def layouts():
    return [layout(), layout(lax.axis_index("lat") == lax.axis_size("lat") - 1)]


def near_rows(near, msg_a, msg_b, rows):
    part = lanes() // SPAN
    places = layouts()
    for side, msg in enumerate((msg_a, msg_b)):
        for n in range(NEAR):
            rows[16 * side + n] = near[side, n]
        for k in range(STEPS):
            x = [msg[k, g] for g in range(GROUPS)]
            for t in range(SETS):
                for p in range(PHASES):
                    column = places[side][p][0]
                    own = gather(x[3 * t], column)
                    for n in (1, 2):
                        own = jnp.where(part == n, gather(x[3 * t + n], column), own)
                    rows[16 * side + NEAR + k, PHASES * t + p] = own


def flat(ref):
    n = 1
    for d in ref.shape[:-1]:
        n *= d
    return ref.reshape((n, LANES))


def east(x):
    return [x[p + 1] if p < PHASES - 1 else pltpu.roll(x[0], LANES - 1, 1) for p in range(PHASES)]


def west(x):
    return [x[p - 1] if p else pltpu.roll(x[PHASES - 1], 1, 1) for p in range(PHASES)]


def weigh(state, count, lo, hi, ground, dense, coef, unroll):
    lane = lanes()
    index = 2 * SPAN + lane - SPAN * (lane // SPAN)
    rows = flat(state)
    blocks = -(-count // 8)
    for b in range(blocks):
        for p in range(PHASES):
            for w in range(2):
                start = (8 * b * VECS + 2 * PHASES + p) * 8 + 2 + w
                x = rows[pl.ds(start, 8, stride=8 * VECS), :]
                ground[PHASES * w + p, 8 * b + 8 : 8 * b + 16, :] = gather(x, index)
    for b in range(blocks):
        con, con_a, con_b, inv, inv_a, inv_b = [
            [ground[PHASES * w + p, 8 * b + 8 + d : 8 * b + 16 + d, :] for p in range(PHASES)]
            for w in range(2)
            for d in (0, 1, -1)
        ]
        f_e = [jnp.sqrt(x * y) for x, y in zip(con, east(con))]
        f_w = west(f_e)
        i_e, i_w = east(inv), west(inv)
        for p in range(PHASES):
            f_a, f_b = jnp.sqrt(con[p] * con_a[p]), jnp.sqrt(con[p] * con_b[p])
            out = (
                1.0 - inv[p] * ((f_e[p] + f_w[p]) + (f_a + f_b)),
                f_e[p] * i_e[p],
                f_w[p] * i_w[p],
                f_a * inv_a[p],
                f_b * inv_b[p],
            )
            for n in range(5):
                dense[5 * p + n, 8 * b : 8 * b + 8, :] = out[n]

    def expand(r, _):
        for n in range(5 * PHASES):
            coef[r, n] = jnp.broadcast_to(dense[n, pl.ds(r, 1), :], TILE)
        return 0

    lax.fori_loop(lo, hi, expand, 0, unroll=unroll)


def advance(row, before, after, coef, c):
    weights = [[coef[c, 5 * p + n] for n in range(5)] for p in range(PHASES)]
    out = []
    for t in range(SETS):
        x = [row(PHASES * t + p) for p in range(PHASES)]
        x_e, x_w = east(x), west(x)
        for p in range(PHASES):
            c0, c_e, c_w, c_a, c_b = weights[p]
            q = PHASES * t + p
            out.append((c0 * x[p] + c_e * x_e[p]) + (c_w * x_w[p] + (c_a * after(q) + c_b * before(q))))
    return out


def finish(row, odd, table, ens_out, clim_out, rows):
    lane = lanes()
    index = 2 * SPAN + (lane + STEPS) // PHASES
    phase = lax.rem(lane + STEPS, PHASES)
    for t in range(SETS):
        blocks = []
        for p in range(PHASES):
            halves = []
            for h in range(2):
                x = jnp.stack([row(8 * h + e, PHASES * t + p) for e in range(8)])
                halves.append(jnp.swapaxes(x, 0, 1))
            blocks.append(jnp.concatenate(halves, axis=1))
        if t == 2:
            for v in range(2):
                halves = []
                for h in range(2):
                    cut = slice(8 * h, 8 * h + 8)
                    x = gather(blocks[0][v, cut], index)
                    for p in range(1, PHASES):
                        x = jnp.where(phase == p, gather(blocks[p][v, cut], index), x)
                    halves.append(x)
                clim_out[v, rows, :] = jnp.concatenate(halves, axis=0)
        lhs = jnp.concatenate([x.astype(BF16).reshape(8 * 16, LANES) for x in blocks], axis=1)
        out = dot(lhs, table[...], 1).astype(BF16)
        for k in range(3 if t < 2 else 2):
            ens_out[pl.ds(8 * (3 * t + k), 8), rows, :] = out[:, LANES * k : LANES * k + LANES].reshape(8, 16, LANES)


FIN = 16 - STEPS
CHUNK = 8


def walk(src, dst, coef, s):
    lo, hi = STEPS + s + 1, STEPS + ROWS - s - 1

    def step(n, _):
        for e in range(CHUNK):
            r = jnp.minimum(lo + n * CHUNK, hi - CHUNK) + e
            out = advance(lambda q: src[r, q], lambda q: src[r - 1, q], lambda q: src[r + 1, q], coef, r)
            for q in range(VECS):
                dst[r, q] = out[q]
        return 0

    lax.fori_loop(0, -(-(hi - lo) // CHUNK), step, 0)


def keep(kept, n, state, s):
    for d in range(2):
        kept[0, n, d] = state[STEPS + s + 1 - d]
        kept[1, n, d] = state[STEPS + ROWS - s - 2 + d]


def start(own, got_1, got_2, table, state, near, kept, fin, coef, second, edge, ground, dense):
    west_first = west_is_first()
    low = lanes() < HALF

    def unpack(r, _):
        a, b = got_1[r], got_2[r]
        w, e = jnp.where(west_first, a, b), jnp.where(west_first, b, a)
        edge[r] = jnp.where(low, w, pltpu.roll(e, HALF, 1))
        edge[r + ROWS // 2] = jnp.where(low, pltpu.roll(w, HALF, 1), e)
        return 0

    lax.fori_loop(0, ROWS // 2, unpack, 0, unroll=8)

    def take(m, _):
        x = edge[pl.ds(m * 16, 16)].reshape(16 * 8, LANES)
        parts = []
        for _ in range(3):
            parts.append(x.astype(BF16))
            x = x - parts[-1].astype(F32)
        lhs = jnp.concatenate(parts, axis=1)
        for t in range(SETS):
            out = dot(lhs, jnp.concatenate([table[t]] * 3, axis=0)).reshape(16, 8, PHASES * LANES)
            for p in range(PHASES):
                q = PHASES * t + p
                rows = pl.ds(m * 16, 16)
                state[pl.ds(STEPS + m * 16, 16), q] = own[rows, q] + out[:, :, LANES * p : LANES * p + LANES]
        return 0

    lax.fori_loop(0, ROWS // 16, take, 0, unroll=4)
    end = STEPS + ROWS
    weigh(state, end, STEPS + 1, end - 1, ground, dense, coef, 8)
    for n in range(NEAR):
        near[0, n] = state[2 * STEPS - n]
        near[1, n] = state[end - NEAR + n]
    for s in range(STEPS):
        src, dst = (state, second) if s % 2 == 0 else (second, state)
        walk(src, dst, coef, s)
        if s < STEPS - 1:
            keep(kept, s, dst, s + 1)
    for n in range(FIN):
        fin[0, n] = state[STEPS + 15 - n]
        fin[1, n] = state[end - 16 + n]


def main(state, table, ens, clim):
    odd = is_odd()

    def tile(m, _):
        def row(n, q):
            r = 16 * m + 16 + n
            return state[STEPS + jnp.where(odd, r, ROWS - 1 - r), q]

        finish(row, odd, table, ens, clim, row_tile(m))
        return 0

    lax.fori_loop(0, ROWS // 16 - 2, tile, 0)


def tail(
    rows_in, kept, fin, rim_1, rim_2, table, ens_main, clim_main, ens, clim,
    one, two, ground, dense, coef, ens_rows, clim_rows, sem,
):
    odd = is_odd()
    done = pl.ds(16, ROWS - 32)
    copies = [
        pltpu.make_async_copy(ens_main, ens.at[:, done, :], sem.at[0]),
        pltpu.make_async_copy(clim_main, clim.at[:, done, :], sem.at[1]),
    ]
    for copy in copies:
        copy.start()
    west_first = west_is_first()
    low = lanes() < HALF
    places = layout()
    for side in range(2):
        for n in range(NEAR):
            one[16 * side + n] = rows_in[16 * side + n]
        for k in range(STEPS):
            r = 16 * side + NEAR + k
            cor = jnp.where(low == west_first, rim_1[side, k], rim_2[side, k])
            for t in range(SETS):
                for p in range(PHASES):
                    _, is_halo, place = places[p]
                    x = gather(cor, place + SETS * STEPS * t)
                    one[r, PHASES * t + p] = jnp.where(is_halo, x, rows_in[r, PHASES * t + p])
    weigh(one, 32, 1, 31, ground, dense, coef, 10)
    for s in range(STEPS):
        src, dst = (one, two) if s % 2 == 0 else (two, one)
        lo = NEAR - 1 - s
        for side in range(2):
            if s:
                src[16 * side + lo - 1] = kept[side, s - 1, 0]
                src[16 * side + lo] = kept[side, s - 1, 1]
        for side in range(2):
            for r in range(16 * side + lo, 16 * side + lo + STEPS):
                out = advance(lambda q: src[r, q], lambda q: src[r - 1, q], lambda q: src[r + 1, q], coef, r)
                for q in range(VECS):
                    dst[r, q] = out[q]
    for side in range(2):
        for n in range(FIN):
            two[16 * side + n] = fin[side, n]
        for n in range(STEPS):
            two[16 * side + FIN + n] = one[16 * side + 1 + n]
        rising = odd if side else ~odd

        def row(n, q):
            return two[16 * side + jnp.where(rising, n, 15 - n), q]

        finish(row, odd, table, ens_rows.at[side], clim_rows.at[side], pl.ds(0, 16))
        rows = row_tile(jnp.where(rising, ROWS // 16 - 1, 0))
        copies += [
            pltpu.make_async_copy(ens_rows.at[side], ens.at[:, rows, :], sem.at[2 + 2 * side]),
            pltpu.make_async_copy(clim_rows.at[side], clim.at[:, rows, :], sem.at[3 + 2 * side]),
        ]
        for copy in copies[-2:]:
            copy.start()
    for copy in copies:
        copy.wait()


def body(n_lon, n_lat, increment, members, climate_spread, diffusivity, inverse_area, land_sea):
    def place(i, l):
        return i % n_lon * n_lat + l

    def route(target):
        pairs = [(i, l, target(i, l)) for i in range(n_lon) for l in range(n_lat)]
        return [(place(i, l), place(*t)) for i, l, t in pairs if t is not None]

    def pair_b(i, l):
        if l == n_lat - 1:
            return (n_lon - 1 - i, l)
        return None if l == 0 else (i, l + 1 if l % 2 else l - 1)

    route_a = route(lambda i, l: (i, l ^ 1))
    route_b = route(pair_b)
    route_1 = route(lambda i, l: (i ^ 1, l))
    route_2 = route(lambda i, l: ((i + (1 if i % 2 else -1)) % n_lon, l))
    table_edge, table_in, table_halo = tables()
    count = members.shape[0] * 2
    arrays = (members.reshape(count, ROWS, LANES), increment, climate_spread, diffusivity, inverse_area, land_sea)
    side = (STEPS, GROUPS, *TILE)
    hbm = [pl.BlockSpec(memory_space=pltpu.HBM)] * 9
    two = (2, ROWS, LANES)
    packed = ((ROWS // 2, *TILE), F32)
    msg_a, msg_b, msg_1, msg_2, mem_v, src_v, into_v, tab_h_v, own = call(
        edges,
        "edges",
        [(side, F32), (side, F32), packed, packed]
        + [((count, ROWS, LANES), BF16), ((6, ROWS, LANES), F32), (table_in.shape, BF16), (table_halo.shape, BF16)]
        + [((ROWS, VECS, *TILE), F32)],
        9,
        [pltpu.VMEM((2, *side), F32), pltpu.VMEM((ROWS, *TILE), F32), pltpu.VMEM(two, F32), pltpu.VMEM(two, F32)]
        + [pltpu.VMEM((ROWS, LANES), d) for d in (F32, F32, jnp.int32)]
        + [pltpu.VMEM(table_edge.shape, BF16), pltpu.SemaphoreType.DMA((12,))],
        limit=6,
        in_specs=hbm,
    )(*[pltpu.with_memory_space_constraint(x, pltpu.HBM) for x in (*arrays, table_edge, table_in, table_halo)])
    got_b = lax.ppermute(msg_b, AXES, route_b)
    got_a = lax.ppermute(msg_a, AXES, route_a)
    got_2 = lax.ppermute(msg_2, AXES, route_2)
    got_1 = lax.ppermute(msg_1, AXES, route_1)
    (own,) = call(spread, "spread", [((ROWS, VECS, *TILE), F32)], 4, limit=5, aliases={3: 0})(
        mem_v, src_v, into_v, own
    )
    got_1, got_2, own = lax.optimization_barrier((got_1, got_2, own))
    vecs = (VECS, *TILE)
    state, near, kept, fin = call(
        start,
        "start",
        [((EXT, *vecs), F32), ((2, NEAR, *vecs), F32), ((2, STEPS - 1, 2, *vecs), F32), ((2, FIN, *vecs), F32)],
        4,
        [pltpu.VMEM((EXT, 5 * PHASES, *TILE), F32), pltpu.VMEM((EXT, *vecs), F32), pltpu.VMEM((ROWS, *TILE), F32)]
        + [pltpu.VMEM((n, EXT + 20, LANES), F32) for n in (2 * PHASES, 5 * PHASES)],
        limit=14,
        cost=(10**11, 10**8),
    )(own, got_1, got_2, tab_h_v)
    got_a, got_b, state = lax.optimization_barrier((got_a, got_b, state))
    (rim,) = call(rim_of_halo, "rim", [((2, STEPS, *TILE), F32)], 2, limit=4)(got_a, got_b)
    rim_1 = lax.ppermute(rim, AXES, route_1)
    rim_2 = lax.ppermute(rim, AXES, route_2)
    full = [((count, ROWS, LANES), BF16), ((2, ROWS, LANES), F32)]
    most = [((count, ROWS - 32, LANES), BF16), ((2, ROWS - 32, LANES), F32)]
    rim, near = lax.optimization_barrier((rim, near))
    (rows,) = call(near_rows, "near_rows", [((32, *vecs), F32)], 3, limit=4)(near, got_a, got_b)
    ens, clim = call(main, "main", most, 2, limit=5)(state, into_v)
    ens, clim = call(
        tail,
        "tail",
        full,
        8,
        [pltpu.VMEM((32, *vecs), F32)] * 2
        + [pltpu.VMEM((n, 48, LANES), F32) for n in (2 * PHASES, 5 * PHASES)]
        + [pltpu.VMEM((32, 5 * PHASES, *TILE), F32)]
        + [pltpu.VMEM((2, count, 16, LANES), BF16), pltpu.VMEM((2, 2, 16, LANES), F32), pltpu.SemaphoreType.DMA((6,))],
        limit=8,
        out_specs=[pl.BlockSpec(memory_space=pltpu.HBM)] * 2,
    )(rows, kept, fin, rim_1, rim_2, into_v, ens, clim)
    return ens.reshape(members.shape), clim


def solution(mesh):
    return jax.shard_map(
        functools.partial(body, mesh.shape["lon"], mesh.shape["lat"]),
        mesh=mesh,
        in_specs=(
            P(None, "lat", "lon"),
            P(None, None, "lat", "lon"),
            P(None, "lat", "lon"),
            P("lat", "lon"),
            P("lat", "lon"),
            P("lat", "lon"),
        ),
        out_specs=(P(None, None, "lat", "lon"), P(None, "lat", "lon")),
        check_vma=False,
    )
```

```python
import functools

import jax
import jax.numpy as jnp
import numpy as np
from jax import lax
from jax.experimental import pallas as pl
from jax.experimental.pallas import tpu as pltpu
from jax.sharding import PartitionSpec as P

STEPS = 6
ENSEMBLE_WEIGHT = 0.8
CLIMATE_WEIGHT = 0.6
ROWS = 64
LANES = 128
GROUPS = 9
PHASES = 4
SETS = 3
SPAN = (LANES + 2 * STEPS) // PHASES
VECS = PHASES * SETS
HALF = LANES // 2
EXT = ROWS + 2 * STEPS
TILE = (8, LANES)
NEAR = STEPS + 1
AXES = ("lon", "lat")
F32 = jnp.float32
BF16 = jnp.bfloat16
MIB = 1024 * 1024


def tables():
    edge = np.zeros((8, LANES, LANES), np.float32)
    for g in range(8):
        for n in range(STEPS):
            edge[g, LANES - STEPS + n, STEPS * g + n] = 1
            edge[g, n, HALF + STEPS * g + n] = 1
    into = np.zeros((SETS, LANES, PHASES, LANES), np.float32)
    for k in range(SETS):
        for c in range(LANES):
            into[k, c, (c + STEPS) % PHASES, SPAN * k + (c + STEPS) // PHASES] = 1
    into = into.reshape(SETS * LANES, PHASES * LANES)
    halo = np.zeros((SETS, LANES, PHASES, LANES), np.float32)
    for g in range(GROUPS):
        for n in range(STEPS):
            for first, e in ((0, n), (HALF, LANES + STEPS + n)):
                halo[g // SETS, first + STEPS * g + n, e % PHASES, SPAN * (g % SETS) + e // PHASES] = 1
    halo = halo.reshape(SETS, LANES, PHASES * LANES)
    return [jnp.asarray(x, BF16) for x in (edge.reshape(4, 2 * LANES, LANES), into, halo)]


def lanes():
    return lax.broadcasted_iota(jnp.int32, TILE, 1)


def gather(x, index):
    return jnp.take_along_axis(x, index, axis=1)


def dot(a, b, side=0):
    return lax.dot_general(a, b, (((1,), (side,)), ((), ())), preferred_element_type=F32)


def is_odd():
    return lax.rem(lax.axis_index("lat"), 2) == 1


def row_tile(index):
    return pl.ds(pl.multiple_of(index * 16, 16), 16)


def vmem(n):
    return [pl.BlockSpec(memory_space=pltpu.VMEM)] * n


def call(kernel, name, outs, n_in, scratch=(), limit=16, cost=(0, 0), in_specs=None, out_specs=None, aliases=None):
    return pl.pallas_call(
        kernel,
        name=name,
        out_shape=[jax.ShapeDtypeStruct(s, d) for s, d in outs],
        in_specs=in_specs or vmem(n_in),
        out_specs=out_specs or vmem(len(outs)),
        scratch_shapes=list(scratch),
        input_output_aliases=aliases or {},
        compiler_params=pltpu.CompilerParams(vmem_limit_bytes=limit * MIB),
        cost_estimate=pl.CostEstimate(flops=cost[0], bytes_accessed=cost[1], transcendentals=0),
    )


def edges(
    mem, inc, clim, dif, inv, land, table, into, tab_h, msg_a, msg_b, msg_1, msg_2, mem_v, src_v, into_v, tab_h_v, own,
    side_rows, rim, inc_v, clim_v, dif_v, inv_v, land_v, table_v, sem,
):
    pairs = [(inc, inc_v), (land, land_v), (clim, clim_v), (dif, dif_v), (inv, inv_v)]
    part = mem.shape[0] // 4
    pairs += [(mem.at[pl.ds(part * n, part)], mem_v.at[pl.ds(part * n, part)]) for n in range(4)]
    pairs += [(table, table_v), (into, into_v), (tab_h, tab_h_v)]
    copies = [pltpu.make_async_copy(a, b, sem.at[n]) for n, (a, b) in enumerate(pairs)]
    for copy in copies:
        copy.start()
    odd = is_odd()
    lane = lanes()
    for copy in copies[:5]:
        copy.wait()
    wet = land_v[...].astype(F32)
    for v in range(2):
        masked = inc_v[v] * wet
        src_v[v] = ENSEMBLE_WEIGHT * masked
        src_v[2 + v] = CLIMATE_WEIGHT * (clim_v[v] * masked)
    src_v[4] = dif_v[...] * wet
    src_v[5] = inv_v[...]
    zero = jnp.zeros(TILE, F32)

    for side in range(2):
        cut = slice(8 * side, 8 * side + 8)
        rows = pl.ds(56 * side, 8)
        pattern = jnp.stack([src_v[0, rows], src_v[1, rows]] * 4)
        for g in range(GROUPS):
            if g < 8:
                if side == 0 and g % 2 == 0:
                    copies[5 + g // 2].wait()
                block = mem_v[8 * g : 8 * g + 8, pl.ds(48 * side, 16), :].astype(F32)[:, cut] * pattern
            else:
                block = jnp.stack([src_v[2 + n, rows] for n in range(4)] + [zero] * 4)
            block = jnp.swapaxes(block, 0, 1)
            for k in range(STEPS):
                side_rows[side, k, g] = block[7 - k if side else k]
    a_side = jnp.where(odd, 0, 1)
    for msg, which in ((msg_a, a_side), (msg_b, 1 - a_side)):
        msg[0 : 8 * STEPS] = side_rows[which, :, 0:8].reshape(8 * STEPS, *TILE)
        for k in range(0, STEPS, 2):
            two = side_rows[which, k, 8] + pltpu.roll(side_rows[which, k + 1, 8], 4, 0)
            msg[8 * STEPS + k // 2] = two

    column = rim_column()
    ensemble = lax.rem(lane, HALF) < 8 * STEPS
    copies[9].wait()
    acc = None
    for q in range(4):
        pair = [mem_v[16 * q + 8 * j : 16 * q + 8 * j + 8].reshape(8 * ROWS, LANES) for j in range(2)]
        x = dot(jnp.concatenate(pair, axis=1), table_v[q])
        acc = x if acc is None else acc + x
    acc = acc.reshape(8, ROWS, LANES)
    for m in range(ROWS // 8):
        cut = slice(8 * m, 8 * m + 8)
        ends = [gather(src_v[f, cut], column) for f in range(6)] + [zero] * 4
        block = [
            jnp.where(ensemble, acc[f, cut] * ends[f % 2], ends[2 + f]) for f in range(8)
        ]
        block = jnp.swapaxes(jnp.stack(block), 0, 1)
        for e in range(8):
            r = 8 * m + e
            rim[jnp.where(odd, r, ROWS - 1 - r)] = block[e]
    first_east = lax.rem(lax.axis_index("lon"), 2) == 0
    low = lane < HALF
    for r in range(ROWS // 2):
        a, b = rim[r], rim[r + ROWS // 2]
        east_two = jnp.where(low, a, pltpu.roll(b, HALF, 1))
        west_two = jnp.where(low, pltpu.roll(a, HALF, 1), b)
        msg_1[r] = jnp.where(first_east, east_two, west_two)
        msg_2[r] = jnp.where(first_east, west_two, east_two)
    for copy in copies[10:]:
        copy.wait()

    @pl.when(first_out())
    def _():
        deal(mem_v, src_v, into_v, own)


def row_groups(msg, k):
    two = msg[8 * STEPS + k // 2]
    return [msg[8 * k + g] for g in range(8)] + [pltpu.roll(two, 4, 0) if k % 2 else two]


def rim_column():
    lane = lanes()
    n = lax.rem(lax.rem(lane, HALF), STEPS)
    return jnp.where(lane < HALF, LANES - STEPS + n, n)


def layout(fold=False):
    lane = lanes()
    part = lane // SPAN
    out = []
    for p in range(PHASES):
        e = PHASES * (lane - SPAN * part) + p
        west, east = e < STEPS, e >= LANES + STEPS
        column = jnp.clip(e - STEPS, 0, LANES - 1)
        column = jnp.where(fold, LANES - 1 - column, column)
        place = STEPS * part + jnp.where(west, e, HALF + jnp.clip(e - LANES - STEPS, 0, STEPS - 1))
        out.append((column, west | east, jnp.minimum(place, LANES - 1 - 2 * SETS * STEPS)))
    return out


def first_out():
    return lax.axis_index("lon") < 4


def spread(mem, src, table, before, state):
    del before

    @pl.when(~first_out())
    def _():
        deal(mem, src, table, state)


def deal(mem, src, table, state):
    odd = is_odd()
    part = lanes() // SPAN
    places = layout()

    def tile(m, _):
        rows = row_tile(m)
        for t in range(SETS):
            n = 3 if t < 2 else 2
            lhs = [mem[pl.ds(8 * (3 * t + k), 8), rows, :].reshape(8 * 16, LANES) for k in range(n)]
            out = dot(jnp.concatenate(lhs, axis=1), table[: n * LANES, :]).reshape(8, 16, PHASES * LANES)
            for p in range(PHASES):
                column, halo, _ = places[p]
                for h in range(2):
                    cut = slice(8 * h, 8 * h + 8)
                    half = pl.ds(pl.multiple_of(m * 16 + 8 * h, 8), 8)
                    weights = [gather(src[v, half], column) for v in range(2)]
                    block = [out[f, cut, LANES * p : LANES * p + LANES] * weights[f % 2] for f in range(8)]
                    if t == 2:
                        own = (part == 2) & ~halo
                        for f in range(4):
                            block[f] = jnp.where(own, gather(src[2 + f, half], column), block[f])
                    block = jnp.swapaxes(jnp.stack(block), 0, 1)
                    for e in range(8):
                        r = m * 16 + 8 * h + e
                        state[jnp.where(odd, r, ROWS - 1 - r), PHASES * t + p] = block[e]
        return 0

    lax.fori_loop(0, ROWS // 16, tile, 0)


def rim_of_halo(msg_a, msg_b, rim):
    fold = lax.axis_index("lat") == lax.axis_size("lat") - 1
    group = lax.rem(lanes(), HALF) // STEPS
    column = rim_column()
    for side, msg in enumerate((msg_a, msg_b)):
        index = jnp.where(fold, LANES - 1 - column, column) if side else column
        for k in range(STEPS):
            x = row_groups(msg, k)
            acc = gather(x[0], index)
            for g in range(1, GROUPS):
                acc = jnp.where(group == g, gather(x[g], index), acc)
            rim[side, k] = acc


def west_is_first():
    return lax.rem(lax.axis_index("lon"), 2) == 1


def layouts():
    return [layout(), layout(lax.axis_index("lat") == lax.axis_size("lat") - 1)]


def near_rows(near, msg_a, msg_b, rows):
    part = lanes() // SPAN
    places = layouts()
    for side, msg in enumerate((msg_a, msg_b)):
        for n in range(NEAR):
            rows[16 * side + n] = near[side, n]
        for k in range(STEPS):
            x = row_groups(msg, k)
            for t in range(SETS):
                for p in range(PHASES):
                    column = places[side][p][0]
                    own = gather(x[3 * t], column)
                    for n in (1, 2):
                        own = jnp.where(part == n, gather(x[3 * t + n], column), own)
                    rows[16 * side + NEAR + k, PHASES * t + p] = own


def flat(ref):
    n = 1
    for d in ref.shape[:-1]:
        n *= d
    return ref.reshape((n, LANES))


def east(x):
    return [x[p + 1] if p < PHASES - 1 else pltpu.roll(x[0], LANES - 1, 1) for p in range(PHASES)]


def west(x):
    return [x[p - 1] if p else pltpu.roll(x[PHASES - 1], 1, 1) for p in range(PHASES)]


def weigh(state, count, lo, hi, ground, dense, coef, unroll):
    lane = lanes()
    index = 2 * SPAN + lane - SPAN * (lane // SPAN)
    rows = flat(state)
    blocks = -(-count // 8)
    for b in range(blocks):
        for p in range(PHASES):
            for w in range(2):
                start = (8 * b * VECS + 2 * PHASES + p) * 8 + 2 + w
                x = rows[pl.ds(start, 8, stride=8 * VECS), :]
                ground[PHASES * w + p, 8 * b + 8 : 8 * b + 16, :] = gather(x, index)
    for b in range(blocks):
        con, con_a, con_b, inv, inv_a, inv_b = [
            [ground[PHASES * w + p, 8 * b + 8 + d : 8 * b + 16 + d, :] for p in range(PHASES)]
            for w in range(2)
            for d in (0, 1, -1)
        ]
        f_e = [jnp.sqrt(x * y) for x, y in zip(con, east(con))]
        f_w = west(f_e)
        i_e, i_w = east(inv), west(inv)
        for p in range(PHASES):
            f_a, f_b = jnp.sqrt(con[p] * con_a[p]), jnp.sqrt(con[p] * con_b[p])
            out = (
                1.0 - inv[p] * ((f_e[p] + f_w[p]) + (f_a + f_b)),
                f_e[p] * i_e[p],
                f_w[p] * i_w[p],
                f_a * inv_a[p],
                f_b * inv_b[p],
            )
            for n in range(5):
                dense[5 * p + n, 8 * b : 8 * b + 8, :] = out[n]

    def expand(r, _):
        for n in range(5 * PHASES):
            coef[r, n] = jnp.broadcast_to(dense[n, pl.ds(r, 1), :], TILE)
        return 0

    lax.fori_loop(lo, hi, expand, 0, unroll=unroll)


def advance(row, before, after, coef, c):
    weights = [[coef[c, 5 * p + n] for n in range(5)] for p in range(PHASES)]
    out = []
    for t in range(SETS):
        x = [row(PHASES * t + p) for p in range(PHASES)]
        x_e, x_w = east(x), west(x)
        for p in range(PHASES):
            c0, c_e, c_w, c_a, c_b = weights[p]
            q = PHASES * t + p
            out.append((c0 * x[p] + c_e * x_e[p]) + (c_w * x_w[p] + (c_a * after(q) + c_b * before(q))))
    return out


def finish(tiles, table):
    lane = lanes()
    index = 2 * SPAN + (lane + STEPS) // PHASES
    phase = lax.rem(lane + STEPS, PHASES)
    for t in range(SETS):
        lhs = []
        for row, _, clim_out, rows in tiles:
            blocks = []
            for p in range(PHASES):
                halves = []
                for h in range(2):
                    x = jnp.stack([row(8 * h + e, PHASES * t + p) for e in range(8)])
                    halves.append(jnp.swapaxes(x, 0, 1))
                blocks.append(jnp.concatenate(halves, axis=1))
            if t == 2:
                for v in range(2):
                    halves = []
                    for h in range(2):
                        cut = slice(8 * h, 8 * h + 8)
                        x = gather(blocks[0][v, cut], index)
                        for p in range(1, PHASES):
                            x = jnp.where(phase == p, gather(blocks[p][v, cut], index), x)
                        halves.append(x)
                    clim_out[v, rows, :] = jnp.concatenate(halves, axis=0)
            lhs.append(jnp.concatenate([x.astype(BF16).reshape(8 * 16, LANES) for x in blocks], axis=1))
        out = dot(jnp.concatenate(lhs, axis=0), table[...], 1).astype(BF16)
        for n, (_, ens_out, _, rows) in enumerate(tiles):
            for k in range(3 if t < 2 else 2):
                x = out[LANES * n : LANES * n + LANES, LANES * k : LANES * k + LANES].reshape(8, 16, LANES)
                ens_out[pl.ds(8 * (3 * t + k), 8), rows, :] = x


FIN = 16 - STEPS
CHUNK = 8


def walk(src, dst, coef, s):
    lo, hi = STEPS + s + 1, STEPS + ROWS - s - 1

    def step(n, _):
        for e in range(CHUNK):
            r = jnp.minimum(lo + n * CHUNK, hi - CHUNK) + e
            out = advance(lambda q: src[r, q], lambda q: src[r - 1, q], lambda q: src[r + 1, q], coef, r)
            for q in range(VECS):
                dst[r, q] = out[q]
        return 0

    lax.fori_loop(0, -(-(hi - lo) // CHUNK), step, 0)


def keep(kept, n, state, s):
    for d in range(2):
        kept[0, n, d] = state[STEPS + s + 1 - d]
        kept[1, n, d] = state[STEPS + ROWS - s - 2 + d]


def start(own, got_1, got_2, table, state, near, kept, fin, coef, second, edge, ground, dense):
    west_first = west_is_first()
    low = lanes() < HALF

    def unpack(r, _):
        a, b = got_1[r], got_2[r]
        w, e = jnp.where(west_first, a, b), jnp.where(west_first, b, a)
        edge[r] = jnp.where(low, w, pltpu.roll(e, HALF, 1))
        edge[r + ROWS // 2] = jnp.where(low, pltpu.roll(w, HALF, 1), e)
        return 0

    lax.fori_loop(0, ROWS // 2, unpack, 0, unroll=8)

    def take(m, _):
        x = edge[pl.ds(m * 16, 16)].reshape(16 * 8, LANES)
        parts = []
        for _ in range(3):
            parts.append(x.astype(BF16))
            x = x - parts[-1].astype(F32)
        lhs = jnp.concatenate(parts, axis=1)
        for t in range(SETS):
            out = dot(lhs, jnp.concatenate([table[t]] * 3, axis=0)).reshape(16, 8, PHASES * LANES)
            for p in range(PHASES):
                q = PHASES * t + p
                rows = pl.ds(m * 16, 16)
                state[pl.ds(STEPS + m * 16, 16), q] = own[rows, q] + out[:, :, LANES * p : LANES * p + LANES]
        return 0

    lax.fori_loop(0, ROWS // 16, take, 0, unroll=4)
    end = STEPS + ROWS
    weigh(state, end, STEPS + 1, end - 1, ground, dense, coef, 8)
    for n in range(NEAR):
        near[0, n] = state[2 * STEPS - n]
        near[1, n] = state[end - NEAR + n]
    for s in range(STEPS):
        src, dst = (state, second) if s % 2 == 0 else (second, state)
        walk(src, dst, coef, s)
        if s < STEPS - 1:
            keep(kept, s, dst, s + 1)
    for n in range(FIN):
        fin[0, n] = state[STEPS + 15 - n]
        fin[1, n] = state[end - 16 + n]


def main(state, table, ens, clim):
    odd = is_odd()

    def row(n, q, m):
        r = 16 * m + 16 + n
        return state[STEPS + jnp.where(odd, r, ROWS - 1 - r), q]

    finish([(functools.partial(row, m=m), ens, clim, pl.ds(16 * m, 16)) for m in range(2)], table)


def tail(
    rows_in, kept, fin, rim_1, rim_2, table, ens_main, clim_main, ens, clim,
    one, two, ground, dense, coef, ens_rows, clim_rows, sem,
):
    odd = is_odd()
    done = pl.ds(16, ROWS - 32)
    copies = [
        pltpu.make_async_copy(ens_main, ens.at[:, done, :], sem.at[0]),
        pltpu.make_async_copy(clim_main, clim.at[:, done, :], sem.at[1]),
    ]
    for copy in copies:
        copy.start()
    west_first = west_is_first()
    low = lanes() < HALF
    places = layout()
    for side in range(2):
        for n in range(NEAR):
            one[16 * side + n] = rows_in[16 * side + n]
        for k in range(STEPS):
            r = 16 * side + NEAR + k
            cor = jnp.where(low == west_first, rim_1[side, k], rim_2[side, k])
            for t in range(SETS):
                for p in range(PHASES):
                    _, is_halo, place = places[p]
                    x = gather(cor, place + SETS * STEPS * t)
                    one[r, PHASES * t + p] = jnp.where(is_halo, x, rows_in[r, PHASES * t + p])
    weigh(one, 32, 1, 31, ground, dense, coef, 10)
    for s in range(STEPS):
        src, dst = (one, two) if s % 2 == 0 else (two, one)
        lo = NEAR - 1 - s
        for side in range(2):
            if s:
                src[16 * side + lo - 1] = kept[side, s - 1, 0]
                src[16 * side + lo] = kept[side, s - 1, 1]
        for side in range(2):
            for r in range(16 * side + lo, 16 * side + lo + STEPS):
                out = advance(lambda q: src[r, q], lambda q: src[r - 1, q], lambda q: src[r + 1, q], coef, r)
                for q in range(VECS):
                    dst[r, q] = out[q]
    for side in range(2):
        for n in range(FIN):
            two[16 * side + n] = fin[side, n]
        for n in range(STEPS):
            two[16 * side + FIN + n] = one[16 * side + 1 + n]
        rising = odd if side else ~odd

        def row(n, q, side=side, rising=rising):
            return two[16 * side + jnp.where(rising, n, 15 - n), q]

        finish([(row, ens_rows.at[side], clim_rows.at[side], pl.ds(0, 16))], table)
        rows = row_tile(jnp.where(rising, ROWS // 16 - 1, 0))
        copies += [
            pltpu.make_async_copy(ens_rows.at[side], ens.at[:, rows, :], sem.at[2 + 2 * side]),
            pltpu.make_async_copy(clim_rows.at[side], clim.at[:, rows, :], sem.at[3 + 2 * side]),
        ]
        for copy in copies[-2:]:
            copy.start()
    for copy in copies:
        copy.wait()


def body(n_lon, n_lat, increment, members, climate_spread, diffusivity, inverse_area, land_sea):
    def place(i, l):
        return i % n_lon * n_lat + l

    def route(target):
        pairs = [(i, l, target(i, l)) for i in range(n_lon) for l in range(n_lat)]
        return [(place(i, l), place(*t)) for i, l, t in pairs if t is not None]

    def pair_b(i, l):
        if l == n_lat - 1:
            return (n_lon - 1 - i, l)
        return None if l == 0 else (i, l + 1 if l % 2 else l - 1)

    route_a = route(lambda i, l: (i, l ^ 1))
    route_b = route(pair_b)
    route_1 = route(lambda i, l: (i ^ 1, l))
    route_2 = route(lambda i, l: ((i + (1 if i % 2 else -1)) % n_lon, l))
    table_edge, table_in, table_halo = tables()
    count = members.shape[0] * 2
    arrays = (members.reshape(count, ROWS, LANES), increment, climate_spread, diffusivity, inverse_area, land_sea)
    side = (STEPS, GROUPS, *TILE)
    message = (8 * STEPS + STEPS // 2, *TILE)
    hbm = [pl.BlockSpec(memory_space=pltpu.HBM)] * 9
    two = (2, ROWS, LANES)
    packed = ((ROWS // 2, *TILE), F32)
    msg_a, msg_b, msg_1, msg_2, mem_v, src_v, into_v, tab_h_v, own = call(
        edges,
        "edges",
        [(message, F32), (message, F32), packed, packed]
        + [((count, ROWS, LANES), BF16), ((6, ROWS, LANES), F32), (table_in.shape, BF16), (table_halo.shape, BF16)]
        + [((ROWS, VECS, *TILE), F32)],
        9,
        [pltpu.VMEM((2, *side), F32), pltpu.VMEM((ROWS, *TILE), F32), pltpu.VMEM(two, F32), pltpu.VMEM(two, F32)]
        + [pltpu.VMEM((ROWS, LANES), d) for d in (F32, F32, jnp.int32)]
        + [pltpu.VMEM(table_edge.shape, BF16), pltpu.SemaphoreType.DMA((12,))],
        limit=6,
        in_specs=hbm,
    )(*[pltpu.with_memory_space_constraint(x, pltpu.HBM) for x in (*arrays, table_edge, table_in, table_halo)])
    got_b = lax.ppermute(msg_b, AXES, route_b)
    got_a = lax.ppermute(msg_a, AXES, route_a)
    got_2 = lax.ppermute(msg_2, AXES, route_2)
    got_1 = lax.ppermute(msg_1, AXES, route_1)
    (own,) = call(spread, "spread", [((ROWS, VECS, *TILE), F32)], 4, limit=5, aliases={3: 0})(
        mem_v, src_v, into_v, own
    )
    got_1, got_2, own = lax.optimization_barrier((got_1, got_2, own))
    vecs = (VECS, *TILE)
    state, near, kept, fin = call(
        start,
        "start",
        [((EXT, *vecs), F32), ((2, NEAR, *vecs), F32), ((2, STEPS - 1, 2, *vecs), F32), ((2, FIN, *vecs), F32)],
        4,
        [pltpu.VMEM((EXT, 5 * PHASES, *TILE), F32), pltpu.VMEM((EXT, *vecs), F32), pltpu.VMEM((ROWS, *TILE), F32)]
        + [pltpu.VMEM((n, EXT + 20, LANES), F32) for n in (2 * PHASES, 5 * PHASES)],
        limit=14,
        cost=(10**11, 10**8),
    )(own, got_1, got_2, tab_h_v)
    got_a, got_b, state = lax.optimization_barrier((got_a, got_b, state))
    (rim,) = call(rim_of_halo, "rim", [((2, STEPS, *TILE), F32)], 2, limit=4)(got_a, got_b)
    rim_1 = lax.ppermute(rim, AXES, route_1)
    rim_2 = lax.ppermute(rim, AXES, route_2)
    full = [((count, ROWS, LANES), BF16), ((2, ROWS, LANES), F32)]
    most = [((count, ROWS - 32, LANES), BF16), ((2, ROWS - 32, LANES), F32)]
    rim, near = lax.optimization_barrier((rim, near))
    (rows,) = call(near_rows, "near_rows", [((32, *vecs), F32)], 3, limit=4)(near, got_a, got_b)
    ens, clim = call(main, "main", most, 2, limit=5)(state, into_v)
    ens, clim = call(
        tail,
        "tail",
        full,
        8,
        [pltpu.VMEM((32, *vecs), F32)] * 2
        + [pltpu.VMEM((n, 48, LANES), F32) for n in (2 * PHASES, 5 * PHASES)]
        + [pltpu.VMEM((32, 5 * PHASES, *TILE), F32)]
        + [pltpu.VMEM((2, count, 16, LANES), BF16), pltpu.VMEM((2, 2, 16, LANES), F32), pltpu.SemaphoreType.DMA((6,))],
        limit=8,
        out_specs=[pl.BlockSpec(memory_space=pltpu.HBM)] * 2,
    )(rows, kept, fin, rim_1, rim_2, into_v, ens, clim)
    return ens.reshape(members.shape), clim


def solution(mesh):
    return jax.shard_map(
        functools.partial(body, mesh.shape["lon"], mesh.shape["lat"]),
        mesh=mesh,
        in_specs=(
            P(None, "lat", "lon"),
            P(None, None, "lat", "lon"),
            P(None, "lat", "lon"),
            P("lat", "lon"),
            P("lat", "lon"),
            P("lat", "lon"),
        ),
        out_specs=(P(None, None, "lat", "lon"), P(None, "lat", "lon")),
        check_vma=False,
    )
```

```python
import functools

import jax
import jax.numpy as jnp
import numpy as np
from jax import lax
from jax.experimental import pallas as pl
from jax.experimental.pallas import tpu as pltpu
from jax.sharding import PartitionSpec as P

STEPS = 6
ENSEMBLE_WEIGHT = 0.8
CLIMATE_WEIGHT = 0.6
ROWS = 64
LANES = 128
GROUPS = 9
PHASES = 4
SETS = 3
SPAN = (LANES + 2 * STEPS) // PHASES
VECS = PHASES * SETS
HALF = LANES // 2
EXT = ROWS + 2 * STEPS
TILE = (8, LANES)
NEAR = STEPS + 1
AXES = ("lon", "lat")
F32 = jnp.float32
BF16 = jnp.bfloat16
MIB = 1024 * 1024


def tables():
    edge = np.zeros((8, LANES, LANES), np.float32)
    for g in range(8):
        for n in range(STEPS):
            edge[g, LANES - STEPS + n, STEPS * g + n] = 1
            edge[g, n, HALF + STEPS * g + n] = 1
    into = np.zeros((SETS, LANES, PHASES, LANES), np.float32)
    for k in range(SETS):
        for c in range(LANES):
            into[k, c, (c + STEPS) % PHASES, SPAN * k + (c + STEPS) // PHASES] = 1
    into = into.reshape(SETS * LANES, PHASES * LANES)
    halo = np.zeros((SETS, LANES, PHASES, LANES), np.float32)
    for g in range(GROUPS):
        for n in range(STEPS):
            for first, e in ((0, n), (HALF, LANES + STEPS + n)):
                halo[g // SETS, first + STEPS * g + n, e % PHASES, SPAN * (g % SETS) + e // PHASES] = 1
    halo = halo.reshape(SETS, LANES, PHASES * LANES)
    return [jnp.asarray(x, BF16) for x in (edge.reshape(4, 2 * LANES, LANES), into, halo)]


def lanes():
    return lax.broadcasted_iota(jnp.int32, TILE, 1)


def gather(x, index):
    return jnp.take_along_axis(x, index, axis=1)


def dot(a, b, side=0):
    return lax.dot_general(a, b, (((1,), (side,)), ((), ())), preferred_element_type=F32)


def is_odd():
    return lax.rem(lax.axis_index("lat"), 2) == 1


def row_tile(index):
    return pl.ds(pl.multiple_of(index * 16, 16), 16)


def vmem(n):
    return [pl.BlockSpec(memory_space=pltpu.VMEM)] * n


def call(kernel, name, outs, n_in, scratch=(), limit=16, cost=(0, 0), in_specs=None, out_specs=None, aliases=None):
    return pl.pallas_call(
        kernel,
        name=name,
        out_shape=[jax.ShapeDtypeStruct(s, d) for s, d in outs],
        in_specs=in_specs or vmem(n_in),
        out_specs=out_specs or vmem(len(outs)),
        scratch_shapes=list(scratch),
        input_output_aliases=aliases or {},
        compiler_params=pltpu.CompilerParams(vmem_limit_bytes=limit * MIB),
        cost_estimate=pl.CostEstimate(flops=cost[0], bytes_accessed=cost[1], transcendentals=0),
    )


def edges(
    mem, inc, clim, dif, inv, land, table, into, tab_h, msg_a, msg_b, msg_1, msg_2, mem_v, src_v, into_v, tab_h_v, own,
    side_rows, rim, inc_v, clim_v, dif_v, inv_v, land_v, table_v, sem,
):
    pairs = [(inc, inc_v), (land, land_v), (clim, clim_v), (dif, dif_v), (inv, inv_v)]
    part = mem.shape[0] // 4
    pairs += [(mem.at[pl.ds(part * n, part)], mem_v.at[pl.ds(part * n, part)]) for n in range(4)]
    pairs += [(table, table_v), (into, into_v), (tab_h, tab_h_v)]
    copies = [pltpu.make_async_copy(a, b, sem.at[n]) for n, (a, b) in enumerate(pairs)]
    for copy in copies:
        copy.start()
    odd = is_odd()
    lane = lanes()
    for copy in copies[:5]:
        copy.wait()
    wet = land_v[...].astype(F32)
    for v in range(2):
        masked = inc_v[v] * wet
        src_v[v] = ENSEMBLE_WEIGHT * masked
        src_v[2 + v] = CLIMATE_WEIGHT * (clim_v[v] * masked)
    src_v[4] = dif_v[...] * wet
    src_v[5] = inv_v[...]
    zero = jnp.zeros(TILE, F32)

    for side in range(2):
        cut = slice(8 * side, 8 * side + 8)
        rows = pl.ds(56 * side, 8)
        pattern = jnp.stack([src_v[0, rows], src_v[1, rows]] * 4)
        for g in range(GROUPS):
            if g < 8:
                if side == 0 and g % 2 == 0:
                    copies[5 + g // 2].wait()
                block = mem_v[8 * g : 8 * g + 8, pl.ds(48 * side, 16), :].astype(F32)[:, cut] * pattern
            else:
                block = jnp.stack([src_v[2 + n, rows] for n in range(4)] + [zero] * 4)
            block = jnp.swapaxes(block, 0, 1)
            for k in range(STEPS):
                side_rows[side, k, g] = block[7 - k if side else k]
    a_side = jnp.where(odd, 0, 1)
    for msg, which in ((msg_a, a_side), (msg_b, 1 - a_side)):
        msg[0 : 8 * STEPS] = side_rows[which, :, 0:8].reshape(8 * STEPS, *TILE)
        for k in range(0, STEPS, 2):
            two = side_rows[which, k, 8] + pltpu.roll(side_rows[which, k + 1, 8], 4, 0)
            msg[8 * STEPS + k // 2] = two

    column = rim_column()
    ensemble = lax.rem(lane, HALF) < 8 * STEPS
    copies[9].wait()
    acc = None
    for q in range(4):
        pair = [mem_v[16 * q + 8 * j : 16 * q + 8 * j + 8].reshape(8 * ROWS, LANES) for j in range(2)]
        x = dot(jnp.concatenate(pair, axis=1), table_v[q])
        acc = x if acc is None else acc + x
    acc = acc.reshape(8, ROWS, LANES)
    for m in range(ROWS // 8):
        cut = slice(8 * m, 8 * m + 8)
        ends = [gather(src_v[f, cut], column) for f in range(6)] + [zero] * 4
        block = [
            jnp.where(ensemble, acc[f, cut] * ends[f % 2], ends[2 + f]) for f in range(8)
        ]
        block = jnp.swapaxes(jnp.stack(block), 0, 1)
        for e in range(8):
            r = 8 * m + e
            rim[jnp.where(odd, r, ROWS - 1 - r)] = block[e]
    first_east = lax.rem(lax.axis_index("lon"), 2) == 0
    low = lane < HALF
    for r in range(ROWS // 2):
        a, b = rim[r], rim[r + ROWS // 2]
        east_two = jnp.where(low, a, pltpu.roll(b, HALF, 1))
        west_two = jnp.where(low, pltpu.roll(a, HALF, 1), b)
        msg_1[r] = jnp.where(first_east, east_two, west_two)
        msg_2[r] = jnp.where(first_east, west_two, east_two)
    for copy in copies[10:]:
        copy.wait()

    @pl.when(first_out())
    def _():
        deal(mem_v, src_v, into_v, own)


def row_groups(msg, k):
    two = msg[8 * STEPS + k // 2]
    return [msg[8 * k + g] for g in range(8)] + [pltpu.roll(two, 4, 0) if k % 2 else two]


def rim_column():
    lane = lanes()
    n = lax.rem(lax.rem(lane, HALF), STEPS)
    return jnp.where(lane < HALF, LANES - STEPS + n, n)


def layout(fold=False):
    lane = lanes()
    part = lane // SPAN
    out = []
    for p in range(PHASES):
        e = PHASES * (lane - SPAN * part) + p
        west, east = e < STEPS, e >= LANES + STEPS
        column = jnp.clip(e - STEPS, 0, LANES - 1)
        column = jnp.where(fold, LANES - 1 - column, column)
        place = STEPS * part + jnp.where(west, e, HALF + jnp.clip(e - LANES - STEPS, 0, STEPS - 1))
        out.append((column, west | east, jnp.minimum(place, LANES - 1 - 2 * SETS * STEPS)))
    return out


def first_out():
    return lax.axis_index("lon") < 4


def spread(mem, src, table, before, state):
    del before

    @pl.when(~first_out())
    def _():
        deal(mem, src, table, state)


def deal(mem, src, table, state):
    odd = is_odd()
    part = lanes() // SPAN
    places = layout()

    def tile(m, _):
        rows = row_tile(m)
        for t in range(SETS):
            n = 3 if t < 2 else 2
            lhs = [mem[pl.ds(8 * (3 * t + k), 8), rows, :].reshape(8 * 16, LANES) for k in range(n)]
            out = dot(jnp.concatenate(lhs, axis=1), table[: n * LANES, :]).reshape(8, 16, PHASES * LANES)
            for p in range(PHASES):
                column, halo, _ = places[p]
                for h in range(2):
                    cut = slice(8 * h, 8 * h + 8)
                    half = pl.ds(pl.multiple_of(m * 16 + 8 * h, 8), 8)
                    weights = [gather(src[v, half], column) for v in range(2)]
                    block = [out[f, cut, LANES * p : LANES * p + LANES] * weights[f % 2] for f in range(8)]
                    if t == 2:
                        own = (part == 2) & ~halo
                        for f in range(4):
                            block[f] = jnp.where(own, gather(src[2 + f, half], column), block[f])
                    block = jnp.swapaxes(jnp.stack(block), 0, 1)
                    for e in range(8):
                        r = m * 16 + 8 * h + e
                        state[jnp.where(odd, r, ROWS - 1 - r), PHASES * t + p] = block[e]
        return 0

    lax.fori_loop(0, ROWS // 16, tile, 0)


def rim_of_halo(msg_a, msg_b, rim):
    fold = lax.axis_index("lat") == lax.axis_size("lat") - 1
    group = lax.rem(lanes(), HALF) // STEPS
    column = rim_column()
    for side, msg in enumerate((msg_a, msg_b)):
        index = jnp.where(fold, LANES - 1 - column, column) if side else column
        for k in range(STEPS):
            x = row_groups(msg, k)
            acc = gather(x[0], index)
            for g in range(1, GROUPS):
                acc = jnp.where(group == g, gather(x[g], index), acc)
            rim[side, k] = acc


def west_is_first():
    return lax.rem(lax.axis_index("lon"), 2) == 1


def layouts():
    return [layout(), layout(lax.axis_index("lat") == lax.axis_size("lat") - 1)]


def near_rows(near, msg_a, msg_b, rows):
    part = lanes() // SPAN
    places = layouts()
    for side, msg in enumerate((msg_a, msg_b)):
        for n in range(NEAR):
            rows[16 * side + n] = near[side, n]
        for k in range(STEPS):
            x = row_groups(msg, k)
            for t in range(SETS):
                for p in range(PHASES):
                    column = places[side][p][0]
                    own = gather(x[3 * t], column)
                    for n in (1, 2):
                        own = jnp.where(part == n, gather(x[3 * t + n], column), own)
                    rows[16 * side + NEAR + k, PHASES * t + p] = own


def flat(ref):
    n = 1
    for d in ref.shape[:-1]:
        n *= d
    return ref.reshape((n, LANES))


def east(x):
    return [x[p + 1] if p < PHASES - 1 else pltpu.roll(x[0], LANES - 1, 1) for p in range(PHASES)]


def west(x):
    return [x[p - 1] if p else pltpu.roll(x[PHASES - 1], 1, 1) for p in range(PHASES)]


def weigh(state, count, lo, hi, ground, dense, coef, unroll, starts=(0,)):
    lane = lanes()
    index = 2 * SPAN + lane - SPAN * (lane // SPAN)
    rows = flat(state)
    blocks = -(-count // 8)
    for b in range(blocks):
        for p in range(PHASES):
            for w in range(2):
                start = (8 * b * VECS + 2 * PHASES + p) * 8 + 2 + w
                x = rows[pl.ds(start, 8, stride=8 * VECS), :]
                ground[PHASES * w + p, 8 * b + 8 : 8 * b + 16, :] = gather(x, index)
    for b in range(blocks):
        con, con_a, con_b, inv, inv_a, inv_b = [
            [ground[PHASES * w + p, 8 * b + 8 + d : 8 * b + 16 + d, :] for p in range(PHASES)]
            for w in range(2)
            for d in (0, 1, -1)
        ]
        f_e = [jnp.sqrt(x * y) for x, y in zip(con, east(con))]
        f_w = west(f_e)
        i_e, i_w = east(inv), west(inv)
        for p in range(PHASES):
            f_a, f_b = jnp.sqrt(con[p] * con_a[p]), jnp.sqrt(con[p] * con_b[p])
            out = (
                1.0 - inv[p] * ((f_e[p] + f_w[p]) + (f_a + f_b)),
                f_e[p] * i_e[p],
                f_w[p] * i_w[p],
                f_a * inv_a[p],
                f_b * inv_b[p],
            )
            for n in range(5):
                dense[5 * p + n, 8 * b : 8 * b + 8, :] = out[n]

    def expand(r, _):
        for n in range(5 * PHASES):
            for first in starts:
                coef[first + r, n] = jnp.broadcast_to(dense[n, pl.ds(first + r, 1), :], TILE)
        return 0

    lax.fori_loop(lo, hi, expand, 0, unroll=unroll)


def advance(row, before, after, coef, c):
    weights = [[coef[c, 5 * p + n] for n in range(5)] for p in range(PHASES)]
    out = []
    for t in range(SETS):
        x = [row(PHASES * t + p) for p in range(PHASES)]
        x_e, x_w = east(x), west(x)
        for p in range(PHASES):
            c0, c_e, c_w, c_a, c_b = weights[p]
            q = PHASES * t + p
            out.append((c0 * x[p] + c_e * x_e[p]) + (c_w * x_w[p] + (c_a * after(q) + c_b * before(q))))
    return out


def finish(tiles, table):
    lane = lanes()
    index = 2 * SPAN + (lane + STEPS) // PHASES
    phase = lax.rem(lane + STEPS, PHASES)
    for t in range(SETS):
        lhs = []
        for row, _, clim_out, rows in tiles:
            blocks = []
            for p in range(PHASES):
                halves = []
                for h in range(2):
                    x = jnp.stack([row(8 * h + e, PHASES * t + p) for e in range(8)])
                    halves.append(jnp.swapaxes(x, 0, 1))
                blocks.append(jnp.concatenate(halves, axis=1))
            if t == 2:
                for v in range(2):
                    halves = []
                    for h in range(2):
                        cut = slice(8 * h, 8 * h + 8)
                        x = gather(blocks[0][v, cut], index)
                        for p in range(1, PHASES):
                            x = jnp.where(phase == p, gather(blocks[p][v, cut], index), x)
                        halves.append(x)
                    clim_out[v, rows, :] = jnp.concatenate(halves, axis=0)
            lhs.append(jnp.concatenate([x.astype(BF16).reshape(8 * 16, LANES) for x in blocks], axis=1))
        out = dot(jnp.concatenate(lhs, axis=0), table[...], 1).astype(BF16)
        for n, (_, ens_out, _, rows) in enumerate(tiles):
            for k in range(3 if t < 2 else 2):
                x = out[LANES * n : LANES * n + LANES, LANES * k : LANES * k + LANES].reshape(8, 16, LANES)
                ens_out[pl.ds(8 * (3 * t + k), 8), rows, :] = x


FIN = 16 - STEPS
CHUNK = 8


def walk(src, dst, coef, s):
    lo, hi = STEPS + s + 1, STEPS + ROWS - s - 1

    def step(n, _):
        for e in range(CHUNK):
            r = jnp.minimum(lo + n * CHUNK, hi - CHUNK) + e
            out = advance(lambda q: src[r, q], lambda q: src[r - 1, q], lambda q: src[r + 1, q], coef, r)
            for q in range(VECS):
                dst[r, q] = out[q]
        return 0

    lax.fori_loop(0, -(-(hi - lo) // CHUNK), step, 0)


def keep(kept, n, state, s):
    for d in range(2):
        kept[0, n, d] = state[STEPS + s + 1 - d]
        kept[1, n, d] = state[STEPS + ROWS - s - 2 + d]


def start(own, got_1, got_2, table, state, near, kept, fin, coef, second, edge, ground, dense):
    west_first = west_is_first()
    low = lanes() < HALF

    def unpack(r, _):
        a, b = got_1[r], got_2[r]
        w, e = jnp.where(west_first, a, b), jnp.where(west_first, b, a)
        edge[r] = jnp.where(low, w, pltpu.roll(e, HALF, 1))
        edge[r + ROWS // 2] = jnp.where(low, pltpu.roll(w, HALF, 1), e)
        return 0

    lax.fori_loop(0, ROWS // 2, unpack, 0, unroll=8)

    def take(m, _):
        x = edge[pl.ds(m * 16, 16)].reshape(16 * 8, LANES)
        parts = []
        for _ in range(3):
            parts.append(x.astype(BF16))
            x = x - parts[-1].astype(F32)
        lhs = jnp.concatenate(parts, axis=1)
        for t in range(SETS):
            out = dot(lhs, jnp.concatenate([table[t]] * 3, axis=0)).reshape(16, 8, PHASES * LANES)
            for p in range(PHASES):
                q = PHASES * t + p
                rows = pl.ds(m * 16, 16)
                state[pl.ds(STEPS + m * 16, 16), q] = own[rows, q] + out[:, :, LANES * p : LANES * p + LANES]
        return 0

    lax.fori_loop(0, ROWS // 16, take, 0, unroll=4)
    end = STEPS + ROWS
    weigh(state, end, STEPS + 1, end - 1, ground, dense, coef, 8)
    for n in range(NEAR):
        near[0, n] = state[2 * STEPS - n]
        near[1, n] = state[end - NEAR + n]
    for s in range(STEPS):
        src, dst = (state, second) if s % 2 == 0 else (second, state)
        walk(src, dst, coef, s)
        if s < STEPS - 1:
            keep(kept, s, dst, s + 1)
    for n in range(FIN):
        fin[0, n] = state[STEPS + 15 - n]
        fin[1, n] = state[end - 16 + n]


def main(state, table, ens, clim):
    odd = is_odd()

    def row(n, q, m):
        r = 16 * m + 16 + n
        return state[STEPS + jnp.where(odd, r, ROWS - 1 - r), q]

    finish([(functools.partial(row, m=m), ens, clim, pl.ds(16 * m, 16)) for m in range(2)], table)


def tail(
    rows_in, kept, fin, rim_1, rim_2, table, ens_main, clim_main, ens, clim,
    one, two, ground, dense, coef, ens_rows, clim_rows, sem,
):
    odd = is_odd()
    done = pl.ds(16, ROWS - 32)
    copies = [
        pltpu.make_async_copy(ens_main, ens.at[:, done, :], sem.at[0]),
        pltpu.make_async_copy(clim_main, clim.at[:, done, :], sem.at[1]),
    ]
    for copy in copies:
        copy.start()
    west_first = west_is_first()
    low = lanes() < HALF
    places = layout()
    for side in range(2):
        for n in range(NEAR):
            one[16 * side + n] = rows_in[16 * side + n]
        for k in range(STEPS):
            r = 16 * side + NEAR + k
            cor = jnp.where(low == west_first, rim_1[side, k], rim_2[side, k])
            for t in range(SETS):
                for p in range(PHASES):
                    _, is_halo, place = places[p]
                    x = gather(cor, place + SETS * STEPS * t)
                    one[r, PHASES * t + p] = jnp.where(is_halo, x, rows_in[r, PHASES * t + p])
    weigh(one, 32, 1, NEAR + STEPS - 1, ground, dense, coef, 11, (0, 16))
    for s in range(STEPS):
        src, dst = (one, two) if s % 2 == 0 else (two, one)
        lo = NEAR - 1 - s
        for side in range(2):
            if s:
                src[16 * side + lo - 1] = kept[side, s - 1, 0]
                src[16 * side + lo] = kept[side, s - 1, 1]
        for side in range(2):
            for r in range(16 * side + lo, 16 * side + lo + STEPS):
                out = advance(lambda q: src[r, q], lambda q: src[r - 1, q], lambda q: src[r + 1, q], coef, r)
                for q in range(VECS):
                    dst[r, q] = out[q]
    for side in range(2):
        for n in range(FIN):
            two[16 * side + n] = fin[side, n]
        for n in range(STEPS):
            two[16 * side + FIN + n] = one[16 * side + 1 + n]
        rising = odd if side else ~odd

        def row(n, q, side=side, rising=rising):
            return two[16 * side + jnp.where(rising, n, 15 - n), q]

        finish([(row, ens_rows.at[side], clim_rows.at[side], pl.ds(0, 16))], table)
        rows = row_tile(jnp.where(rising, ROWS // 16 - 1, 0))
        copies += [
            pltpu.make_async_copy(ens_rows.at[side], ens.at[:, rows, :], sem.at[2 + 2 * side]),
            pltpu.make_async_copy(clim_rows.at[side], clim.at[:, rows, :], sem.at[3 + 2 * side]),
        ]
        for copy in copies[-2:]:
            copy.start()
    for copy in copies:
        copy.wait()


def body(n_lon, n_lat, increment, members, climate_spread, diffusivity, inverse_area, land_sea):
    def place(i, l):
        return i % n_lon * n_lat + l

    def route(target):
        pairs = [(i, l, target(i, l)) for i in range(n_lon) for l in range(n_lat)]
        return [(place(i, l), place(*t)) for i, l, t in pairs if t is not None]

    def pair_b(i, l):
        if l == n_lat - 1:
            return (n_lon - 1 - i, l)
        return None if l == 0 else (i, l + 1 if l % 2 else l - 1)

    route_a = route(lambda i, l: (i, l ^ 1))
    route_b = route(pair_b)
    route_1 = route(lambda i, l: (i ^ 1, l))
    route_2 = route(lambda i, l: ((i + (1 if i % 2 else -1)) % n_lon, l))
    table_edge, table_in, table_halo = tables()
    count = members.shape[0] * 2
    arrays = (members.reshape(count, ROWS, LANES), increment, climate_spread, diffusivity, inverse_area, land_sea)
    side = (STEPS, GROUPS, *TILE)
    message = (8 * STEPS + STEPS // 2, *TILE)
    hbm = [pl.BlockSpec(memory_space=pltpu.HBM)] * 9
    two = (2, ROWS, LANES)
    packed = ((ROWS // 2, *TILE), F32)
    msg_a, msg_b, msg_1, msg_2, mem_v, src_v, into_v, tab_h_v, own = call(
        edges,
        "edges",
        [(message, F32), (message, F32), packed, packed]
        + [((count, ROWS, LANES), BF16), ((6, ROWS, LANES), F32), (table_in.shape, BF16), (table_halo.shape, BF16)]
        + [((ROWS, VECS, *TILE), F32)],
        9,
        [pltpu.VMEM((2, *side), F32), pltpu.VMEM((ROWS, *TILE), F32), pltpu.VMEM(two, F32), pltpu.VMEM(two, F32)]
        + [pltpu.VMEM((ROWS, LANES), d) for d in (F32, F32, jnp.int32)]
        + [pltpu.VMEM(table_edge.shape, BF16), pltpu.SemaphoreType.DMA((12,))],
        limit=6,
        in_specs=hbm,
    )(*[pltpu.with_memory_space_constraint(x, pltpu.HBM) for x in (*arrays, table_edge, table_in, table_halo)])
    got_b = lax.ppermute(msg_b, AXES, route_b)
    got_a = lax.ppermute(msg_a, AXES, route_a)
    got_2 = lax.ppermute(msg_2, AXES, route_2)
    got_1 = lax.ppermute(msg_1, AXES, route_1)
    (own,) = call(spread, "spread", [((ROWS, VECS, *TILE), F32)], 4, limit=5, aliases={3: 0})(
        mem_v, src_v, into_v, own
    )
    got_1, got_2, own = lax.optimization_barrier((got_1, got_2, own))
    vecs = (VECS, *TILE)
    state, near, kept, fin = call(
        start,
        "start",
        [((EXT, *vecs), F32), ((2, NEAR, *vecs), F32), ((2, STEPS - 1, 2, *vecs), F32), ((2, FIN, *vecs), F32)],
        4,
        [pltpu.VMEM((EXT, 5 * PHASES, *TILE), F32), pltpu.VMEM((EXT, *vecs), F32), pltpu.VMEM((ROWS, *TILE), F32)]
        + [pltpu.VMEM((n, EXT + 20, LANES), F32) for n in (2 * PHASES, 5 * PHASES)],
        limit=14,
        cost=(10**11, 10**8),
    )(own, got_1, got_2, tab_h_v)
    got_a, got_b, state = lax.optimization_barrier((got_a, got_b, state))
    (rim,) = call(rim_of_halo, "rim", [((2, STEPS, *TILE), F32)], 2, limit=4)(got_a, got_b)
    rim_1 = lax.ppermute(rim, AXES, route_1)
    rim_2 = lax.ppermute(rim, AXES, route_2)
    full = [((count, ROWS, LANES), BF16), ((2, ROWS, LANES), F32)]
    most = [((count, ROWS - 32, LANES), BF16), ((2, ROWS - 32, LANES), F32)]
    rim, near = lax.optimization_barrier((rim, near))
    (rows,) = call(near_rows, "near_rows", [((32, *vecs), F32)], 3, limit=4)(near, got_a, got_b)
    ens, clim = call(main, "main", most, 2, limit=5)(state, into_v)
    ens, clim = call(
        tail,
        "tail",
        full,
        8,
        [pltpu.VMEM((32, *vecs), F32)] * 2
        + [pltpu.VMEM((n, 48, LANES), F32) for n in (2 * PHASES, 5 * PHASES)]
        + [pltpu.VMEM((32, 5 * PHASES, *TILE), F32)]
        + [pltpu.VMEM((2, count, 16, LANES), BF16), pltpu.VMEM((2, 2, 16, LANES), F32), pltpu.SemaphoreType.DMA((6,))],
        limit=8,
        out_specs=[pl.BlockSpec(memory_space=pltpu.HBM)] * 2,
    )(rows, kept, fin, rim_1, rim_2, into_v, ens, clim)
    return ens.reshape(members.shape), clim


def solution(mesh):
    return jax.shard_map(
        functools.partial(body, mesh.shape["lon"], mesh.shape["lat"]),
        mesh=mesh,
        in_specs=(
            P(None, "lat", "lon"),
            P(None, None, "lat", "lon"),
            P(None, "lat", "lon"),
            P("lat", "lon"),
            P("lat", "lon"),
            P("lat", "lon"),
        ),
        out_specs=(P(None, None, "lat", "lon"), P(None, "lat", "lon")),
        check_vma=False,
    )
```
